32 devices in a mesh: dp: 2 (over y), tm: 16 (over z, x, core).
Axes of the slice: x: 2, y: 2, z: 4, core: 2. Of those that a mesh axis runs over, the one named last changes fastest.
Arguments:
- signal: bfloat16 [2, 16384, 256], P('dp', 'tm'), may hold values from -6 to 6
- cotangent: bfloat16 [2, 16384, 256], P('dp', 'tm'), may hold values from -6 to 6
- first_history_weight: bfloat16 [256, 512], replicated, may hold values from -0.25 to 0.25
- first_current_weight: bfloat16 [256, 512], replicated, may hold values from -0.25 to 0.25
- first_residual_weight: bfloat16 [256, 256], replicated, may hold values from -0.375 to 0.375
- second_history_weight: bfloat16 [256, 512], replicated, may hold values from -0.25 to 0.25
- second_current_weight: bfloat16 [256, 512], replicated, may hold values from -0.25 to 0.25
- second_residual_weight: bfloat16 [256, 256], replicated, may hold values from -0.375 to 0.375
Outputs:
- grad_signal: bfloat16 [2, 16384, 256], P('dp', 'tm')
- grad_past_one: bfloat16 [256, 512], replicated
- grad_now_one: bfloat16 [256, 512], replicated
- grad_mix_one: bfloat16 [256, 256], replicated
- grad_past_two: bfloat16 [256, 512], replicated
- grad_now_two: bfloat16 [256, 512], replicated
- grad_mix_two: bfloat16 [256, 256], replicated
The draws below stay inside these ranges and needn't reach their ends.
All inputs are finite; a program needn't handle non-finite values.
Results may differ from the reference program's by a relative error of at most 0.0068.
Values may be sent and summed in bfloat16 or wider, within the bound.
A program may use at most 64 MiB of HBM per device.

```python
import math
import jax
import jax.numpy as jnp
from jax import lax

RES = 256
GATE = 512
FIRST_DILATION = 512
SECOND_DILATION = 8192
BATCH = 2
LENGTH = 16384


def steps_of(own_key, extent, shards, smallest, high):
    level = 1.0
    for axis_at, blocks in shards:
        steps = jax.random.uniform(jax.random.fold_in(jax.random.fold_in(own_key, 6), axis_at), (blocks,), jnp.float32, smallest / len(shards), high / len(shards))
        level = level * jnp.repeat(jnp.exp(steps), extent[axis_at] // blocks).reshape((-1,) + (1,) * (len(extent) - 1 - axis_at))
    return level


def noise(key, dims, width, limit, cuts=(), kind=jnp.bfloat16):
    array = width * jax.random.normal(key, dims, jnp.float32)
    if cuts:
        array = array * steps_of(key, dims, cuts, -0.22, 0.18)
    return jnp.clip(array, -limit, limit).astype(kind)


def setup_inputs(seed: int = 0) -> dict:
    keys = jax.random.split(jax.random.key(seed), 9)
    return {
        "signal": noise(keys[0], (BATCH, LENGTH, RES), 1.0, 6.0, ((0, 2), (1, 16))),
        "cotangent": noise(keys[1], (BATCH, LENGTH, RES), 1.0, 6.0, ((0, 2), (1, 16))),
        "first_history_weight": noise(keys[2], (RES, GATE), (2 * RES) ** -0.5, 0.25),
        "first_current_weight": noise(keys[3], (RES, GATE), (2 * RES) ** -0.5, 0.25),
        "first_residual_weight": noise(keys[4], (GATE // 2, RES), (GATE // 2) ** -0.5, 0.375),
        "second_history_weight": noise(keys[5], (RES, GATE), (2 * RES) ** -0.5, 0.25),
        "second_current_weight": noise(keys[6], (RES, GATE), (2 * RES) ** -0.5, 0.25),
        "second_residual_weight": noise(keys[7], (GATE // 2, RES), (GATE // 2) ** -0.5, 0.375),
    }


def gated_layer_forward(input_traces, tap_past, tap_now, mixing, dilation):
    zero_rows = jnp.zeros((dilation, input_traces.shape[1]), input_traces.dtype)
    past_rows = jnp.concatenate([zero_rows, input_traces[:-dilation]], axis=0)
    pre_act = jnp.dot(past_rows, tap_past, preferred_element_type=jnp.float32) + jnp.dot(input_traces, tap_now, preferred_element_type=jnp.float32)
    half_width = pre_act.shape[1] // 2
    filter_part = jnp.tanh(pre_act[:, :half_width])
    gate_part = jax.nn.sigmoid(pre_act[:, half_width:])
    hidden = (filter_part * gate_part).astype(jnp.bfloat16)
    output = (input_traces.astype(jnp.float32) + jnp.dot(hidden, mixing, preferred_element_type=jnp.float32)).astype(jnp.bfloat16)
    return (past_rows, filter_part, gate_part, hidden, output)

def gated_layer_backward(input_traces, saved, incoming_gradient, tap_past, tap_now, mixing, dilation):
    past_rows, filter_part, gate_part, hidden, output = saved
    hidden_grad = jnp.dot(incoming_gradient, mixing.T, preferred_element_type=jnp.float32)
    filter_grad = hidden_grad * gate_part * (1.0 - filter_part * filter_part)
    gate_grad = hidden_grad * filter_part * gate_part * (1.0 - gate_part)
    pre_grad = jnp.concatenate([filter_grad, gate_grad], axis=1).astype(jnp.bfloat16)
    past_term = jnp.dot(past_rows.T, pre_grad, preferred_element_type=jnp.float32)
    now_term = jnp.dot(input_traces.T, pre_grad, preferred_element_type=jnp.float32)
    mix_term = jnp.dot(hidden.T, incoming_gradient, preferred_element_type=jnp.float32)
    ahead_rows = jnp.dot(pre_grad, tap_past.T, preferred_element_type=jnp.float32).astype(jnp.bfloat16)
    zero_rows = jnp.zeros((dilation, ahead_rows.shape[1]), ahead_rows.dtype)
    trailing_later_rows = jnp.concatenate([ahead_rows[dilation:], zero_rows], axis=0)
    input_grad = (incoming_gradient.astype(jnp.float32) + jnp.dot(pre_grad, tap_now.T, preferred_element_type=jnp.float32) + trailing_later_rows.astype(jnp.float32)).astype(jnp.bfloat16)
    return (input_grad, (past_term, now_term, mix_term))

def finish_term(stacked, scale_factor):
    return (lax.optimization_barrier(jnp.sum(stacked, axis=0)) * scale_factor).astype(jnp.bfloat16)

def reference(signal, cotangent, first_history_weight, first_current_weight, first_residual_weight, second_history_weight, second_current_weight, second_residual_weight):

    def one_sequence(pair):
        input_traces, incoming_gradient = pair
        first_layer_stash = gated_layer_forward(input_traces, first_history_weight, first_current_weight, first_residual_weight, FIRST_DILATION)
        hidden_activation = first_layer_stash[4]
        second_layer_stash = gated_layer_forward(hidden_activation, second_history_weight, second_current_weight, second_residual_weight, SECOND_DILATION)
        hidden_gradient, second_layer_terms = gated_layer_backward(hidden_activation, second_layer_stash, incoming_gradient, second_history_weight, second_current_weight, second_residual_weight, SECOND_DILATION)
        input_gradient, first_layer_terms = gated_layer_backward(input_traces, first_layer_stash, hidden_gradient, first_history_weight, first_current_weight, first_residual_weight, FIRST_DILATION)
        return (input_gradient, first_layer_terms, second_layer_terms)
    grad_signal, first_layer_terms, second_layer_terms = lax.map(one_sequence, (signal, cotangent))
    scale_factor = 1.0 / math.sqrt(BATCH * LENGTH)
    return (grad_signal, finish_term(first_layer_terms[0], scale_factor), finish_term(first_layer_terms[1], scale_factor), finish_term(first_layer_terms[2], scale_factor), finish_term(second_layer_terms[0], scale_factor), finish_term(second_layer_terms[1], scale_factor), finish_term(second_layer_terms[2], scale_factor))
```

```python
import functools
import math

import jax
import jax.numpy as jnp
from jax import lax
from jax.experimental import pallas as pl
from jax.experimental.pallas import tpu as pltpu
from jax.sharding import PartitionSpec as P

FIRST_DILATION = 512
SECOND_DILATION = 8192
MESH = pl.DeviceIdType.MESH
F32 = jnp.float32
BF16 = jnp.bfloat16


def mm(a, b):
    return lax.dot_general(a, b, (((1,), (0,)), ((), ())), preferred_element_type=F32)


def mm_nt(a, b):
    return lax.dot_general(a, b, (((1,), (1,)), ((), ())), preferred_element_type=F32)


def mm_tn(a, b):
    return lax.dot_general(a, b, (((0,), (0,)), ((), ())), preferred_element_type=F32)


def sigmoid(x):
    return 0.5 * jnp.tanh(0.5 * x) + 0.5


def kernel(
    count, offset, steps, chunks,
    sig, cot, p1, w1, m1, p2, w2, m2,
    gsig, tp1, tn1, tm1, tp2, tn2, tm2,
    halo, f1, g1, h1, mid, past2, ahead2, back2, pre2, hg2, loc2, ahead1, back1, loc1,
    halo_s, halo_r, mid_s, mid_r, a2_s, a2_r, a1_s, a1_r,
):
    d1 = FIRST_DILATION
    c = sig.shape[1]
    me = lax.axis_index("tm")
    has_prev, has_next = me > 0, me < count - 1
    has_far, has_near = me < count - offset, me >= offset
    nxt, prv = lax.rem(me + 1, count), lax.rem(me + count - 1, count)
    far, near = lax.rem(me + offset, count), lax.rem(me + count - offset, count)

    barrier = pltpu.get_barrier_semaphore()
    for there, target in ((has_prev, prv), (has_next, nxt), (has_far, far), (has_near, near)):
        @pl.when(there)
        def _(target=target):
            pl.semaphore_signal(barrier, inc=1, device_id={"tm": target}, device_id_type=MESH)
    peers = sum(there.astype(jnp.int32) for there in (has_prev, has_next, has_far, has_near))
    pl.semaphore_wait(barrier, peers)

    def copy(src, dst, s, r, target):
        return pltpu.make_async_remote_copy(
            src_ref=src, dst_ref=dst, send_sem=s, recv_sem=r, device_id={"tm": target}, device_id_type=MESH
        )

    halo_copy = copy(sig.at[pl.ds(steps - d1, d1)], halo, halo_s, halo_r, nxt)
    mid_copy, a2_copy, a1_copy = [], [], []
    for i, (at, size) in enumerate(chunks):
        rows = pl.ds(at, size)
        mid_copy.append(copy(mid.at[rows], past2.at[rows], mid_s.at[i], mid_r.at[i], far))
        a2_copy.append(copy(ahead2.at[rows], back2.at[rows], a2_s.at[i], a2_r.at[i], near))
        a1_copy.append(copy(ahead1.at[rows], back1.at[rows], a1_s.at[i], a1_r.at[i], prv) if at < d1 else None)

    @pl.when(has_next)
    def _():
        halo_copy.start()

    @pl.when(jnp.logical_not(has_prev))
    def _():
        halo[...] = jnp.zeros_like(halo)

    @pl.when(jnp.logical_not(has_near))
    def _():
        past2[...] = jnp.zeros_like(past2)

    @pl.when(jnp.logical_not(has_far))
    def _():
        back2[...] = jnp.zeros_like(back2)

    @pl.when(jnp.logical_not(has_next))
    def _():
        back1[...] = jnp.zeros_like(back1)

    def past1(at, size):
        return halo[pl.ds(at, size), :] if at < d1 else sig[pl.ds(at - d1, size), :]

    def add(ref, first, value):
        ref[...] = value if first else ref[...] + value

    waited_halo = False
    for i, (at, size) in enumerate(chunks):
        rows = pl.ds(at, size)
        if at < d1 and not waited_halo:
            waited_halo = True

            @pl.when(has_prev)
            def _():
                halo_copy.wait_recv()
        u = sig[rows, :]
        pre = mm(past1(at, size), p1[...]) + mm(u, w1[...])
        f = jnp.tanh(pre[:, :c])
        g = sigmoid(pre[:, c:])
        hid = (f * g).astype(BF16)
        f1[rows, :] = f
        g1[rows, :] = g
        h1[rows, :] = hid
        mid[rows, :] = (u.astype(F32) + mm(hid, m1[...])).astype(BF16)

        @pl.when(has_far)
        def _(i=i):
            mid_copy[i].start()

    for at, size in chunks:
        rows = pl.ds(at, size)
        pre2[rows, :] = mm(mid[rows, :], w2[...])
        hg2[rows, :] = mm_nt(cot[rows, :], m2[...])

    def second(i):
        at, size = chunks[i]
        rows = pl.ds(at, size)

        @pl.when(has_near)
        def _():
            mid_copy[i].wait_recv()
        past = past2[rows, :]
        up = cot[rows, :]
        pre = mm(past, p2[...]) + pre2[rows, :]
        f = jnp.tanh(pre[:, :c])
        g = sigmoid(pre[:, c:])
        hid = (f * g).astype(BF16)
        hg = hg2[rows, :]
        pg = jnp.concatenate([hg * g * (1.0 - f * f), hg * f * g * (1.0 - g)], axis=1).astype(BF16)

        @pl.when(has_near)
        def _():
            ahead2[rows, :] = mm_nt(pg, p2[...]).astype(BF16)
            a2_copy[i].start()
        loc2[rows, :] = up.astype(F32) + mm_nt(pg, w2[...])
        add(tp2, i == 0, mm_tn(past, pg))
        add(tn2, i == 0, mm_tn(mid[rows, :], pg))
        add(tm2, i == 0, mm_tn(hid, up))

    def first(i):
        at, size = chunks[i]
        rows = pl.ds(at, size)

        @pl.when(has_far)
        def _():
            a2_copy[i].wait_recv()
        up = (loc2[rows, :] + back2[rows, :].astype(F32)).astype(BF16)
        hg = mm_nt(up, m1[...])
        f, g = f1[rows, :], g1[rows, :]
        pg = jnp.concatenate([hg * g * (1.0 - f * f), hg * f * g * (1.0 - g)], axis=1).astype(BF16)
        ahead1[rows, :] = mm_nt(pg, p1[...]).astype(BF16)
        if at < d1:
            @pl.when(has_prev)
            def _():
                a1_copy[i].start()
        loc1[rows, :] = up.astype(F32) + mm_nt(pg, w1[...])
        add(tp1, i == 0, mm_tn(past1(at, size), pg))
        add(tn1, i == 0, mm_tn(sig[rows, :], pg))
        add(tm1, i == 0, mm_tn(h1[rows, :], up))

    second(0)
    for i in range(1, len(chunks)):
        second(i)
        first(i - 1)
    first(len(chunks) - 1)

    for i, (at, size) in enumerate(chunks):
        if at < d1:
            @pl.when(has_next)
            def _(i=i):
                a1_copy[i].wait_recv()
    local = steps - d1
    if local:
        gsig[pl.ds(0, local), :] = (loc1[pl.ds(0, local), :] + ahead1[pl.ds(d1, local), :].astype(F32)).astype(BF16)
    gsig[pl.ds(local, d1), :] = (loc1[pl.ds(local, d1), :] + back1[...].astype(F32)).astype(BF16)

    @pl.when(has_next)
    def _():
        halo_copy.wait_send()
    for i in range(len(chunks)):
        @pl.when(has_far)
        def _(i=i):
            mid_copy[i].wait_send()

        @pl.when(has_near)
        def _(i=i):
            a2_copy[i].wait_send()
        if a1_copy[i] is not None:
            @pl.when(has_prev)
            def _(i=i):
                a1_copy[i].wait_send()


def body(signal, cotangent, p1, w1, m1, p2, w2, m2):
    seqs, steps, c = signal.shape
    count = lax.axis_size("tm")
    gate = p1.shape[1]
    scale = 1.0 / math.sqrt(seqs * lax.axis_size("dp") * steps * count)
    chunks = ((512, 256), (0, 256), (256, 256), (768, 128), (896, 128))
    nch = len(chunks)
    vm = pl.BlockSpec(memory_space=pltpu.VMEM)
    S = jax.ShapeDtypeStruct
    dma = pltpu.SemaphoreType.DMA
    terms = [S((c, gate), F32), S((c, gate), F32), S((c, c), F32)]
    out = pl.pallas_call(
        functools.partial(kernel, count, SECOND_DILATION // steps, steps, chunks),
        out_shape=[S((steps, c), BF16)] + terms + terms,
        in_specs=[vm] * 8,
        out_specs=[vm] * 7,
        scratch_shapes=[
            pltpu.VMEM((FIRST_DILATION, c), BF16),
            pltpu.VMEM((steps, c), F32),
            pltpu.VMEM((steps, c), F32),
            pltpu.VMEM((steps, c), BF16),
            pltpu.VMEM((steps, c), BF16),
            pltpu.VMEM((steps, c), BF16),
            pltpu.VMEM((steps, c), BF16),
            pltpu.VMEM((steps, c), BF16),
            pltpu.VMEM((steps, gate), F32),
            pltpu.VMEM((steps, c), F32),
            pltpu.VMEM((steps, c), F32),
            pltpu.VMEM((steps, c), BF16),
            pltpu.VMEM((FIRST_DILATION, c), BF16),
            pltpu.VMEM((steps, c), F32),
            dma, dma,
            dma((nch,)), dma((nch,)), dma((nch,)), dma((nch,)), dma((nch,)), dma((nch,)),
        ],
        compiler_params=pltpu.CompilerParams(
            collective_id=0, has_side_effects=True, vmem_limit_bytes=48 * 1024 * 1024
        ),
        name="layers",
    )(signal.reshape(steps, c), cotangent.reshape(steps, c), p1, w1, m1, p2, w2, m2)
    summed = lax.psum(tuple(out[1:]), ("dp", "tm"))
    grads = tuple((t * scale).astype(BF16) for t in summed)
    return (out[0].reshape(signal.shape),) + grads


def solution(mesh):
    in_specs = (P("dp", "tm", None), P("dp", "tm", None), P(), P(), P(), P(), P(), P())
    out_specs = (P("dp", "tm", None), P(), P(), P(), P(), P(), P())
    return jax.shard_map(body, mesh=mesh, in_specs=in_specs, out_specs=out_specs, check_vma=False)
```

```python
import functools
import math

import jax
import jax.numpy as jnp
from jax import lax
from jax.experimental import pallas as pl
from jax.experimental.pallas import tpu as pltpu
from jax.sharding import PartitionSpec as P

FIRST_DILATION = 512
SECOND_DILATION = 8192
MESH = pl.DeviceIdType.MESH
F32 = jnp.float32
BF16 = jnp.bfloat16


def mm(a, b):
    return lax.dot_general(a, b, (((1,), (0,)), ((), ())), preferred_element_type=F32)


def mm_nt(a, b):
    return lax.dot_general(a, b, (((1,), (1,)), ((), ())), preferred_element_type=F32)


def mm_tn(a, b):
    return lax.dot_general(a, b, (((0,), (0,)), ((), ())), preferred_element_type=F32)


def sigmoid(x):
    return 0.5 * jnp.tanh(0.5 * x) + 0.5


class Sum:
    def __init__(self, acc, pack, got1, got2, got3, sum1, sum2, res, ss, rs, scale):
        self.acc, self.pack, self.got1, self.got2, self.got3 = acc, pack, got1, got2, got3
        self.sum1, self.sum2, self.res, self.ss, self.rs, self.scale = sum1, sum2, res, ss, rs, scale
        half = acc.shape[0] // 2
        quarter, piece = half // 4, half // 16
        self.half, self.quarter, self.piece = half, quarter, piece
        dp, me = lax.axis_index("dp"), lax.axis_index("tm")
        q, p, z, partner, plane, column = places(dp, me)
        self.mine = pl.multiple_of(q * half, half)
        self.other = pl.multiple_of((1 - q) * half, half)
        self.base2 = pl.multiple_of(q * half + p * quarter, quarter)
        self.base3 = pl.multiple_of(q * half + p * quarter + z * piece, piece)
        self.own2 = pl.multiple_of(p * quarter, quarter)
        self.own3 = pl.multiple_of(z * piece, piece)
        sem = iter(range(14))

        def copy(src, dst, target):
            i = next(sem)
            return pltpu.make_async_remote_copy(
                src_ref=src, dst_ref=dst, send_sem=ss.at[i], recv_sem=rs.at[i], device_id=target, device_id_type=MESH
            )

        self.c1 = [copy(pack, got1, partner)]
        self.c2 = []
        for r, (there, place) in enumerate(plane):
            rows = pl.ds(pl.multiple_of(place * quarter, quarter), quarter)
            self.c2.append(copy(sum1.at[rows], got2.at[r], there))
        self.c3 = []
        for r, (there, place) in enumerate(column):
            rows = pl.ds(pl.multiple_of(place * piece, piece), piece)
            self.c3.append(copy(sum2.at[rows], got3.at[r], there))
        three, two = res.at[pl.ds(self.base3, piece)], res.at[pl.ds(self.base2, quarter)]
        one = res.at[pl.ds(self.mine, half)]
        self.g3 = [copy(three, three, there) for there, _ in column]
        self.g2 = [copy(two, two, there) for there, _ in plane]
        self.g1 = [copy(one, one, partner)]

    def add(self, first, past, now, mix):
        for at, value in ((0, past), (4, now), (8, mix)):
            if value is None:
                continue
            for j in range(value.shape[1] // 128):
                rows = pl.ds((at + j) * value.shape[0], value.shape[0])
                part = value[:, j * 128 : (j + 1) * 128]
                self.acc[rows, :] = part if first else self.acc[rows, :] + part

    def start(self, copies):
        for c in copies:
            c.start()

    def arrive(self, copies):
        for c in copies:
            c.wait_recv()

    def send1(self):
        self.pack[...] = self.acc[pl.ds(self.other, self.half), :].astype(BF16)
        self.start(self.c1)

    def send2(self):
        self.arrive(self.c1)
        total = self.acc[pl.ds(self.mine, self.half), :] + self.got1[...].astype(F32)
        self.acc[pl.ds(self.mine, self.half), :] = total
        self.sum1[...] = total.astype(BF16)
        self.start(self.c2)

    def send3(self):
        self.arrive(self.c2)
        total = self.acc[pl.ds(self.base2, self.quarter), :]
        for r in range(3):
            total = total + self.got2[r].astype(F32)
        self.acc[pl.ds(self.base2, self.quarter), :] = total
        self.sum2[...] = total.astype(BF16)
        self.start(self.c3)

    def back3(self):
        self.arrive(self.c3)
        total = self.acc[pl.ds(self.base3, self.piece), :]
        for r in range(3):
            total = total + self.got3[r].astype(F32)
        self.res[pl.ds(self.base3, self.piece), :] = (total * self.scale).astype(BF16)
        self.start(self.g3)

    def back2(self):
        self.arrive(self.g3)
        self.start(self.g2)

    def back1(self):
        self.arrive(self.g2)
        self.start(self.g1)

    def finish(self):
        self.arrive(self.g1)

    def drain(self):
        for c in self.c1 + self.c2 + self.c3 + self.g3 + self.g2 + self.g1:
            c.wait_send()


class Local(Sum):
    def __init__(self, acc):
        self.acc = acc

    def nothing(self):
        pass

    send1 = send2 = send3 = back3 = back2 = back1 = finish = drain = nothing


def places(dp, me):
    q, x, z = lax.rem(me, 2), lax.rem(lax.div(me, 2), 2), lax.div(me, 4)
    z0, z1 = lax.rem(z, 2), lax.div(z, 2)
    partner = {"dp": dp, "tm": me + 1 - 2 * q}
    plane, column = [], []
    for r in (1, 2, 3):
        lo, hi = r % 2, r // 2
        xx = x + lo * (1 - 2 * x)
        yy = dp + hi * (1 - 2 * dp)
        plane.append(({"dp": yy, "tm": me + 2 * (xx - x)}, yy * 2 + xx))
        zz = z + lo * (1 - 2 * z0) + 2 * hi * (1 - 2 * z1)
        column.append(({"dp": dp, "tm": me + 4 * (zz - z)}, zz))
    return q, dp * 2 + x, z, partner, plane, column


def kernel(count, offset, steps, chunks, scale, fused, *refs):
    hbm, refs = refs[:8], refs[8:]
    results, refs = refs[:3], refs[3:]
    vmem, refs = refs[:8], refs[8:]
    gsig, out1, out2, store, refs = refs[0], refs[1], refs[2], refs[3], refs[4:]
    stores = [pltpu.make_async_copy(src, dst, store.at[i]) for i, (src, dst) in enumerate(zip((gsig, out1, out2), results))]
    halo, f1, g1, h1, mid, past2, ahead2, back2, pre2, hg2, loc2, ahead1, back1, loc1 = refs[:14]
    load, halo_s, halo_r, mid_s, mid_r, a2_s, a2_r, a1_s, a1_r = refs[14:23]
    sig, cot, p1, w1, m1, p2, w2, m2 = vmem
    loads = {}
    for i, (src, dst) in enumerate(zip(hbm, vmem)):
        loads[i] = pltpu.make_async_copy(src, dst, load.at[i])
    for i in (0, 3, 2, 4, 6, 1, 7, 5):
        loads[i].start()

    d1 = FIRST_DILATION
    c = sig.shape[1]
    me = lax.axis_index("tm")
    has_prev, has_next = me > 0, me < count - 1
    has_far, has_near = me < count - offset, me >= offset
    nxt, prv = lax.rem(me + 1, count), lax.rem(me + count - 1, count)
    far, near = lax.rem(me + offset, count), lax.rem(me + count - offset, count)

    barrier = pltpu.get_barrier_semaphore()
    peers = sum(there.astype(jnp.int32) for there in (has_prev, has_next, has_far, has_near))
    for there, target in ((has_prev, prv), (has_next, nxt), (has_far, far), (has_near, near)):
        @pl.when(there)
        def _(target=target):
            pl.semaphore_signal(barrier, inc=1, device_id={"tm": target}, device_id_type=MESH)
    if fused:
        _, _, _, partner, plane, column = places(lax.axis_index("dp"), me)
        for target in [partner] + [there for there, _ in plane + column]:
            pl.semaphore_signal(barrier, inc=1, device_id=target, device_id_type=MESH)
        peers = peers + 7
    pl.semaphore_wait(barrier, peers)
    if fused:
        per = refs[23:]
        sum_one = Sum(*per[:7], out1, *per[7:9], scale)
        sum_two = Sum(*per[9:16], out2, *per[16:18], scale)
    else:
        sum_one, sum_two = Local(out1), Local(out2)

    def copy(src, dst, s, r, target):
        return pltpu.make_async_remote_copy(
            src_ref=src, dst_ref=dst, send_sem=s, recv_sem=r, device_id={"tm": target}, device_id_type=MESH
        )

    halo_copy = copy(hbm[0].at[pl.ds(steps - d1, d1)], halo, halo_s, halo_r, nxt)
    mid_copy, a2_copy, a1_copy = [], [], []
    for i, (at, size) in enumerate(chunks):
        rows = pl.ds(at, size)
        mid_copy.append(copy(mid.at[rows], past2.at[rows], mid_s.at[i], mid_r.at[i], far))
        a2_copy.append(copy(ahead2.at[rows], back2.at[rows], a2_s.at[i], a2_r.at[i], near))
        a1_copy.append(copy(ahead1.at[rows], back1.at[rows], a1_s.at[i], a1_r.at[i], prv) if at < d1 else None)

    @pl.when(has_next)
    def _():
        halo_copy.start()

    @pl.when(jnp.logical_not(has_prev))
    def _():
        halo[...] = jnp.zeros_like(halo)

    @pl.when(jnp.logical_not(has_near))
    def _():
        past2[...] = jnp.zeros_like(past2)

    @pl.when(jnp.logical_not(has_far))
    def _():
        back2[...] = jnp.zeros_like(back2)

    @pl.when(jnp.logical_not(has_next))
    def _():
        back1[...] = jnp.zeros_like(back1)

    def past1(at, size):
        return halo[pl.ds(at, size), :] if at < d1 else sig[pl.ds(at - d1, size), :]

    for i in (0, 3, 2, 4):
        loads[i].wait()
    waited_halo = False
    for i, (at, size) in enumerate(chunks):
        rows = pl.ds(at, size)
        if at < d1 and not waited_halo:
            waited_halo = True

            @pl.when(has_prev)
            def _():
                halo_copy.wait_recv()
        u = sig[rows, :]
        pre = mm(past1(at, size), p1[...]) + mm(u, w1[...])
        f = jnp.tanh(pre[:, :c])
        g = sigmoid(pre[:, c:])
        hid = (f * g).astype(BF16)
        f1[rows, :] = f
        g1[rows, :] = g
        h1[rows, :] = hid
        mid[rows, :] = (u.astype(F32) + mm(hid, m1[...])).astype(BF16)

        @pl.when(has_far)
        def _(i=i):
            mid_copy[i].start()

    for i in (6, 1, 7, 5):
        loads[i].wait()
    for at, size in chunks:
        rows = pl.ds(at, size)
        pre2[rows, :] = mm(mid[rows, :], w2[...])
        hg2[rows, :] = mm_nt(cot[rows, :], m2[...])

    def second(i):
        at, size = chunks[i]
        rows = pl.ds(at, size)

        @pl.when(has_near)
        def _():
            mid_copy[i].wait_recv()
        past = past2[rows, :]
        up = cot[rows, :]
        pre = mm(past, p2[...]) + pre2[rows, :]
        f = jnp.tanh(pre[:, :c])
        g = sigmoid(pre[:, c:])
        hid = (f * g).astype(BF16)
        hg = hg2[rows, :]
        pg = jnp.concatenate([hg * g * (1.0 - f * f), hg * f * g * (1.0 - g)], axis=1).astype(BF16)

        @pl.when(has_near)
        def _():
            ahead2[rows, :] = mm_nt(pg, p2[...]).astype(BF16)
            a2_copy[i].start()
        loc2[rows, :] = up.astype(F32) + mm_nt(pg, w2[...])
        sum_two.add(i == 0, mm_tn(past, pg), mm_tn(mid[rows, :], pg), mm_tn(hid, up))

    def first(i):
        at, size = chunks[i]
        rows = pl.ds(at, size)

        @pl.when(has_far)
        def _():
            a2_copy[i].wait_recv()
        up = (loc2[rows, :] + back2[rows, :].astype(F32)).astype(BF16)
        hg = mm_nt(up, m1[...])
        f, g = f1[rows, :], g1[rows, :]
        pg = jnp.concatenate([hg * g * (1.0 - f * f), hg * f * g * (1.0 - g)], axis=1).astype(BF16)
        def terms():
            sum_one.add(i == 0, mm_tn(past1(at, size), pg), mm_tn(sig[rows, :], pg), mm_tn(h1[rows, :], up))

        def grads():
            ahead1[rows, :] = mm_nt(pg, p1[...]).astype(BF16)
            if at < d1:
                @pl.when(has_prev)
                def _():
                    a1_copy[i].start()
            loc1[rows, :] = up.astype(F32) + mm_nt(pg, w1[...])

        if i < last:
            grads()
            terms()
        else:
            terms()
            sum_one.send1()
            grads()

    last = len(chunks) - 1
    second(0)
    for i in range(1, last):
        second(i)
        first(i - 1)
    second(last)
    sum_two.send1()
    first(last - 1)
    sum_two.send2()
    sum_two.send3()
    first(last)
    sum_two.back3()
    sum_one.send2()
    sum_two.back2()

    for i, (at, size) in enumerate(chunks):
        if at < d1:
            @pl.when(has_next)
            def _(i=i):
                a1_copy[i].wait_recv()
    local = steps - d1
    if local:
        gsig[pl.ds(0, local), :] = (loc1[pl.ds(0, local), :] + ahead1[pl.ds(d1, local), :].astype(F32)).astype(BF16)
    gsig[pl.ds(local, d1), :] = (loc1[pl.ds(local, d1), :] + back1[...].astype(F32)).astype(BF16)
    stores[0].start()

    sum_one.send3()
    sum_two.back1()
    sum_one.back3()
    sum_one.back2()
    sum_two.finish()
    stores[2].start()
    sum_one.back1()
    sum_one.finish()
    stores[1].start()
    sum_one.drain()
    sum_two.drain()

    for c in stores:
        c.wait()

    @pl.when(has_next)
    def _():
        halo_copy.wait_send()
    for i in range(len(chunks)):
        @pl.when(has_far)
        def _(i=i):
            mid_copy[i].wait_send()

        @pl.when(has_near)
        def _(i=i):
            a2_copy[i].wait_send()
        if a1_copy[i] is not None:
            @pl.when(has_prev)
            def _(i=i):
                a1_copy[i].wait_send()


def write(gs, one, two, gsig, gp1, gn1, gm1, gp2, gn2, gm2, sem):
    copies = [pltpu.make_async_copy(gs, gsig, sem.at[20])]
    for k, (packed, outs) in enumerate(((one, (gp1, gn1, gm1)), (two, (gp2, gn2, gm2)))):
        block = 0
        for out in outs:
            height = out.shape[0]
            for j in range(out.shape[1] // 128):
                src = packed.at[pl.ds(block * height, height)]
                copies.append(pltpu.make_async_copy(src, out.at[:, pl.ds(j * 128, 128)], sem.at[k * 10 + block]))
                block += 1
    for c in copies:
        c.start()
    for c in copies:
        c.wait()


def body(signal, cotangent, p1, w1, m1, p2, w2, m2):
    seqs, steps, c = signal.shape
    count, groups = lax.axis_size("tm"), lax.axis_size("dp")
    gate = p1.shape[1]
    scale = 1.0 / math.sqrt(seqs * groups * steps * count)
    fused = (groups, count) == (2, 16)
    chunks = ((512, 256), (0, 256), (256, 256), (768, 128), (896, 128))
    nch = len(chunks)
    hbm = pl.BlockSpec(memory_space=pltpu.HBM)
    S = jax.ShapeDtypeStruct
    dma = pltpu.SemaphoreType.DMA
    wide = (2 * gate + c) // 128 * c
    packed = S((wide, 128), BF16 if fused else F32)
    args = (signal.reshape(steps, c), cotangent.reshape(steps, c), p1, w1, m1, p2, w2, m2)
    half = wide // 2
    per_sum = [
        pltpu.VMEM((wide, 128), F32),
        pltpu.VMEM((half, 128), BF16),
        pltpu.VMEM((half, 128), BF16),
        pltpu.VMEM((3, half // 4, 128), BF16),
        pltpu.VMEM((3, half // 16, 128), BF16),
        pltpu.VMEM((half, 128), BF16),
        pltpu.VMEM((half // 4, 128), BF16),
        dma((14,)),
        dma((14,)),
    ]
    gs, one, two = pl.pallas_call(
        functools.partial(kernel, count, SECOND_DILATION // steps, steps, chunks, scale, fused),
        out_shape=[S((steps, c), BF16), packed, packed],
        in_specs=[hbm] * 8,
        out_specs=[hbm] * 3,
        scratch_shapes=[pltpu.VMEM(a.shape, BF16) for a in args]
        + [
            pltpu.VMEM((steps, c), BF16),
            pltpu.VMEM(packed.shape, packed.dtype),
            pltpu.VMEM(packed.shape, packed.dtype),
            dma((3,)),
            pltpu.VMEM((FIRST_DILATION, c), BF16),
            pltpu.VMEM((steps, c), F32),
            pltpu.VMEM((steps, c), F32),
            pltpu.VMEM((steps, c), BF16),
            pltpu.VMEM((steps, c), BF16),
            pltpu.VMEM((steps, c), BF16),
            pltpu.VMEM((steps, c), BF16),
            pltpu.VMEM((steps, c), BF16),
            pltpu.VMEM((steps, gate), F32),
            pltpu.VMEM((steps, c), F32),
            pltpu.VMEM((steps, c), F32),
            pltpu.VMEM((steps, c), BF16),
            pltpu.VMEM((FIRST_DILATION, c), BF16),
            pltpu.VMEM((steps, c), F32),
            dma((8,)),
            dma, dma,
            dma((nch,)), dma((nch,)), dma((nch,)), dma((nch,)), dma((nch,)), dma((nch,)),
        ]
        + (per_sum * 2 if fused else []),
        compiler_params=pltpu.CompilerParams(
            collective_id=0, has_side_effects=True, vmem_limit_bytes=62 * 1024 * 1024
        ),
        name="layers",
    )(*args)
    if not fused:
        one, two = lax.psum((one, two), ("dp", "tm"))
        one, two = (one * scale).astype(BF16), (two * scale).astype(BF16)
    shapes = [S((steps, c), BF16)] + [S((c, gate), BF16), S((c, gate), BF16), S((c, c), BF16)] * 2
    out = pl.pallas_call(
        write,
        out_shape=shapes,
        in_specs=[hbm] * 3,
        out_specs=[hbm] * 7,
        scratch_shapes=[dma((21,))],
        compiler_params=pltpu.CompilerParams(vmem_limit_bytes=62 * 1024 * 1024),
        name="write",
    )(gs, one, two)
    return (out[0].reshape(signal.shape),) + tuple(out[1:])


def solution(mesh):
    in_specs = (P("dp", "tm", None), P("dp", "tm", None), P(), P(), P(), P(), P(), P())
    out_specs = (P("dp", "tm", None), P(), P(), P(), P(), P(), P())
    return jax.shard_map(body, mesh=mesh, in_specs=in_specs, out_specs=out_specs, check_vma=False)
```

```python
import functools
import math

import jax
import jax.numpy as jnp
from jax import lax
from jax.experimental import pallas as pl
from jax.experimental.pallas import tpu as pltpu
from jax.sharding import PartitionSpec as P

FIRST_DILATION = 512
SECOND_DILATION = 8192
MESH = pl.DeviceIdType.MESH
F32 = jnp.float32
BF16 = jnp.bfloat16


def mm(a, b):
    return lax.dot_general(a, b, (((1,), (0,)), ((), ())), preferred_element_type=F32)


def mm_nt(a, b):
    return lax.dot_general(a, b, (((1,), (1,)), ((), ())), preferred_element_type=F32)


def mm_tn(a, b):
    return lax.dot_general(a, b, (((0,), (0,)), ((), ())), preferred_element_type=F32)


def sigmoid(x):
    return 0.5 * jnp.tanh(0.5 * x) + 0.5


class Sum:
    def __init__(self, acc, pack, got1, got2, got3, sum1, sum2, res, ss, rs, scale):
        self.acc, self.pack, self.got1, self.got2, self.got3 = acc, pack, got1, got2, got3
        self.sum1, self.sum2, self.res, self.ss, self.rs, self.scale = sum1, sum2, res, ss, rs, scale
        half = acc.shape[0] // 2
        quarter, piece = half // 4, half // 16
        self.half, self.quarter, self.piece = half, quarter, piece
        dp, me = lax.axis_index("dp"), lax.axis_index("tm")
        q, p, z, partner, plane, column = places(dp, me)
        self.mine = pl.multiple_of(q * half, half)
        self.other = pl.multiple_of((1 - q) * half, half)
        self.base2 = pl.multiple_of(q * half + p * quarter, quarter)
        self.base3 = pl.multiple_of(q * half + p * quarter + z * piece, piece)
        self.own2 = pl.multiple_of(p * quarter, quarter)
        self.own3 = pl.multiple_of(z * piece, piece)
        sem = iter(range(14))

        def copy(src, dst, target):
            i = next(sem)
            return pltpu.make_async_remote_copy(
                src_ref=src, dst_ref=dst, send_sem=ss.at[i], recv_sem=rs.at[i], device_id=target, device_id_type=MESH
            )

        self.c1 = [copy(pack, got1, partner)]
        self.c2 = []
        for r, (there, place) in enumerate(plane):
            rows = pl.ds(pl.multiple_of(place * quarter, quarter), quarter)
            self.c2.append(copy(sum1.at[rows], got2.at[r], there))
        self.c3 = []
        for r, (there, place) in enumerate(column):
            rows = pl.ds(pl.multiple_of(place * piece, piece), piece)
            self.c3.append(copy(sum2.at[rows], got3.at[r], there))
        three, two = res.at[pl.ds(self.base3, piece)], res.at[pl.ds(self.base2, quarter)]
        one = res.at[pl.ds(self.mine, half)]
        self.g3 = [copy(three, three, there) for there, _ in column]
        self.g2 = [copy(two, two, there) for there, _ in plane]
        self.g1 = [copy(one, one, partner)]

    def add(self, first, past, now, mix):
        for at, value in ((0, past), (4, now), (8, mix)):
            if value is None:
                continue
            for j in range(value.shape[1] // 128):
                rows = pl.ds((at + j) * value.shape[0], value.shape[0])
                part = value[:, j * 128 : (j + 1) * 128]
                self.acc[rows, :] = part if first else self.acc[rows, :] + part

    def start(self, copies):
        for c in copies:
            c.start()

    def arrive(self, copies):
        for c in copies:
            c.wait_recv()

    def send1(self):
        self.pack[...] = self.acc[pl.ds(self.other, self.half), :].astype(BF16)
        self.start(self.c1)

    def send2(self):
        self.arrive(self.c1)
        total = self.acc[pl.ds(self.mine, self.half), :] + self.got1[...].astype(F32)
        self.acc[pl.ds(self.mine, self.half), :] = total
        self.sum1[...] = total.astype(BF16)
        self.start(self.c2)

    def send3(self):
        self.arrive(self.c2)
        total = self.acc[pl.ds(self.base2, self.quarter), :]
        for r in range(3):
            total = total + self.got2[r].astype(F32)
        self.acc[pl.ds(self.base2, self.quarter), :] = total
        self.sum2[...] = total.astype(BF16)
        self.start(self.c3)

    def back3(self):
        self.arrive(self.c3)
        total = self.acc[pl.ds(self.base3, self.piece), :]
        for r in range(3):
            total = total + self.got3[r].astype(F32)
        self.res[pl.ds(self.base3, self.piece), :] = (total * self.scale).astype(BF16)
        self.start(self.g3)

    def back2(self):
        self.arrive(self.g3)
        self.start(self.g2)

    def back1(self):
        self.arrive(self.g2)
        self.start(self.g1)

    def finish(self):
        self.arrive(self.g1)

    def drain(self):
        for c in self.c1 + self.c2 + self.c3 + self.g3 + self.g2 + self.g1:
            c.wait_send()


class Local(Sum):
    def __init__(self, acc):
        self.acc = acc

    def nothing(self):
        pass

    send1 = send2 = send3 = back3 = back2 = back1 = finish = drain = nothing


def places(dp, me):
    q, x, z = lax.rem(me, 2), lax.rem(lax.div(me, 2), 2), lax.div(me, 4)
    z0, z1 = lax.rem(z, 2), lax.div(z, 2)
    partner = {"dp": dp, "tm": me + 1 - 2 * q}
    plane, column = [], []
    for r in (1, 2, 3):
        lo, hi = r % 2, r // 2
        xx = x + lo * (1 - 2 * x)
        yy = dp + hi * (1 - 2 * dp)
        plane.append(({"dp": yy, "tm": me + 2 * (xx - x)}, yy * 2 + xx))
        zz = z + lo * (1 - 2 * z0) + 2 * hi * (1 - 2 * z1)
        column.append(({"dp": dp, "tm": me + 4 * (zz - z)}, zz))
    return q, dp * 2 + x, z, partner, plane, column


def kernel(count, offset, steps, chunks, scale, fused, *refs):
    hbm, refs = refs[:8], refs[8:]
    results, refs = refs[:7], refs[7:]
    vmem, refs = refs[:8], refs[8:]
    local, out1, out2, store, refs = refs[:7], refs[7], refs[8], refs[9], refs[10:]
    gsig = local[0]
    stores = [pltpu.make_async_copy(src, dst, store.at[i]) for i, (src, dst) in enumerate(zip(local, results))]

    def unpack(packed, first):
        block = 0
        for i in range(first, first + 3):
            height, width = local[i].shape
            for j in range(width // 128):
                local[i][:, j * 128 : (j + 1) * 128] = packed[pl.ds(block * height, height), :]
                block += 1
            stores[i].start()
    halo, f1, g1, h1, mid, past2, ahead2, back2, pre2, hg2, loc2, ahead1, back1, loc1 = refs[:14]
    load, halo_s, halo_r, mid_s, mid_r, a2_s, a2_r, a1_s, a1_r = refs[14:23]
    sig, cot, p1, w1, m1, p2, w2, m2 = vmem
    loads = {}
    for i, (src, dst) in enumerate(zip(hbm, vmem)):
        loads[i] = pltpu.make_async_copy(src, dst, load.at[i])
    for i in (0, 3, 2, 4, 6, 1, 7, 5):
        loads[i].start()

    d1 = FIRST_DILATION
    c = sig.shape[1]
    me = lax.axis_index("tm")
    has_prev, has_next = me > 0, me < count - 1
    has_far, has_near = me < count - offset, me >= offset
    nxt, prv = lax.rem(me + 1, count), lax.rem(me + count - 1, count)
    far, near = lax.rem(me + offset, count), lax.rem(me + count - offset, count)

    barrier = pltpu.get_barrier_semaphore()
    peers = sum(there.astype(jnp.int32) for there in (has_prev, has_next, has_far, has_near))
    for there, target in ((has_prev, prv), (has_next, nxt), (has_far, far), (has_near, near)):
        @pl.when(there)
        def _(target=target):
            pl.semaphore_signal(barrier, inc=1, device_id={"tm": target}, device_id_type=MESH)
    if fused:
        _, _, _, partner, plane, column = places(lax.axis_index("dp"), me)
        for target in [partner] + [there for there, _ in plane + column]:
            pl.semaphore_signal(barrier, inc=1, device_id=target, device_id_type=MESH)
        peers = peers + 7
    pl.semaphore_wait(barrier, peers)
    if fused:
        per = refs[23:]
        sum_one = Sum(*per[:7], out1, *per[7:9], scale)
        sum_two = Sum(*per[9:16], out2, *per[16:18], scale)
    else:
        sum_one, sum_two = Local(out1), Local(out2)

    def copy(src, dst, s, r, target):
        return pltpu.make_async_remote_copy(
            src_ref=src, dst_ref=dst, send_sem=s, recv_sem=r, device_id={"tm": target}, device_id_type=MESH
        )

    halo_copy = copy(hbm[0].at[pl.ds(steps - d1, d1)], halo, halo_s, halo_r, nxt)
    mid_copy, a2_copy, a1_copy = [], [], []
    for i, (at, size) in enumerate(chunks):
        rows = pl.ds(at, size)
        mid_copy.append(copy(mid.at[rows], past2.at[rows], mid_s.at[i], mid_r.at[i], far))
        a2_copy.append(copy(ahead2.at[rows], back2.at[rows], a2_s.at[i], a2_r.at[i], near))
        a1_copy.append(copy(ahead1.at[rows], back1.at[rows], a1_s.at[i], a1_r.at[i], prv) if at < d1 else None)

    @pl.when(has_next)
    def _():
        halo_copy.start()

    @pl.when(jnp.logical_not(has_prev))
    def _():
        halo[...] = jnp.zeros_like(halo)

    @pl.when(jnp.logical_not(has_near))
    def _():
        past2[...] = jnp.zeros_like(past2)

    @pl.when(jnp.logical_not(has_far))
    def _():
        back2[...] = jnp.zeros_like(back2)

    @pl.when(jnp.logical_not(has_next))
    def _():
        back1[...] = jnp.zeros_like(back1)

    def past1(at, size):
        return halo[pl.ds(at, size), :] if at < d1 else sig[pl.ds(at - d1, size), :]

    for i in (0, 3, 2, 4):
        loads[i].wait()
    def send_middle(i):
        @pl.when(has_far)
        def _():
            if i >= 2:
                mid_copy[i - 2].wait_send()
            mid_copy[i].start()

    waited_halo = False
    for i, (at, size) in enumerate(chunks):
        rows = pl.ds(at, size)
        if at < d1 and not waited_halo:
            waited_halo = True

            @pl.when(has_prev)
            def _():
                halo_copy.wait_recv()
        u = sig[rows, :]
        pre = mm(past1(at, size), p1[...]) + mm(u, w1[...])
        f = jnp.tanh(pre[:, :c])
        g = sigmoid(pre[:, c:])
        hid = (f * g).astype(BF16)
        f1[rows, :] = f
        g1[rows, :] = g
        h1[rows, :] = hid
        mid[rows, :] = (u.astype(F32) + mm(hid, m1[...])).astype(BF16)

        if i < 2:
            send_middle(i)

    for i in (6, 1, 7, 5):
        loads[i].wait()
    for at, size in chunks:
        rows = pl.ds(at, size)
        pre2[rows, :] = mm(mid[rows, :], w2[...])
        hg2[rows, :] = mm_nt(cot[rows, :], m2[...])

    def second(i):
        at, size = chunks[i]
        rows = pl.ds(at, size)

        @pl.when(has_near)
        def _():
            mid_copy[i].wait_recv()
        past = past2[rows, :]
        up = cot[rows, :]
        pre = mm(past, p2[...]) + pre2[rows, :]
        f = jnp.tanh(pre[:, :c])
        g = sigmoid(pre[:, c:])
        hid = (f * g).astype(BF16)
        hg = hg2[rows, :]
        pg = jnp.concatenate([hg * g * (1.0 - f * f), hg * f * g * (1.0 - g)], axis=1).astype(BF16)

        @pl.when(has_near)
        def _():
            ahead2[rows, :] = mm_nt(pg, p2[...]).astype(BF16)
            a2_copy[i].start()
        loc2[rows, :] = up.astype(F32) + mm_nt(pg, w2[...])
        sum_two.add(i == 0, mm_tn(past, pg), mm_tn(mid[rows, :], pg), mm_tn(hid, up))

    def first(i):
        at, size = chunks[i]
        rows = pl.ds(at, size)

        @pl.when(has_far)
        def _():
            a2_copy[i].wait_recv()
        up = (loc2[rows, :] + back2[rows, :].astype(F32)).astype(BF16)
        hg = mm_nt(up, m1[...])
        f, g = f1[rows, :], g1[rows, :]
        pg = jnp.concatenate([hg * g * (1.0 - f * f), hg * f * g * (1.0 - g)], axis=1).astype(BF16)
        def terms():
            sum_one.add(i == 0, mm_tn(past1(at, size), pg), mm_tn(sig[rows, :], pg), mm_tn(h1[rows, :], up))

        def grads():
            ahead1[rows, :] = mm_nt(pg, p1[...]).astype(BF16)
            if at < d1:
                @pl.when(has_prev)
                def _():
                    a1_copy[i].start()
            loc1[rows, :] = up.astype(F32) + mm_nt(pg, w1[...])

        if i < last:
            grads()
            terms()
        else:
            terms()
            sum_one.send1()
            grads()

    last = len(chunks) - 1
    second(0)
    send_middle(2)
    second(1)
    send_middle(3)
    second(2)
    send_middle(4)
    first(0)
    second(3)
    first(1)
    second(4)
    sum_two.send1()
    first(2)
    sum_two.send2()
    first(last - 1)
    sum_two.send3()
    first(last)
    sum_two.back3()
    sum_one.send2()
    sum_two.back2()

    for i, (at, size) in enumerate(chunks):
        if at < d1:
            @pl.when(has_next)
            def _(i=i):
                a1_copy[i].wait_recv()
    rest = steps - d1
    if rest:
        gsig[pl.ds(0, rest), :] = (loc1[pl.ds(0, rest), :] + ahead1[pl.ds(d1, rest), :].astype(F32)).astype(BF16)
    gsig[pl.ds(rest, d1), :] = (loc1[pl.ds(rest, d1), :] + back1[...].astype(F32)).astype(BF16)
    stores[0].start()

    sum_one.send3()
    sum_two.back1()
    sum_one.back3()
    sum_one.back2()
    sum_two.finish()
    unpack(out2, 4)
    sum_one.back1()
    sum_one.finish()
    unpack(out1, 1)
    sum_one.drain()
    sum_two.drain()

    for c in stores:
        c.wait()

    @pl.when(has_next)
    def _():
        halo_copy.wait_send()
    for i in range(len(chunks)):
        if i >= len(chunks) - 2:
            @pl.when(has_far)
            def _(i=i):
                mid_copy[i].wait_send()

        @pl.when(has_near)
        def _(i=i):
            a2_copy[i].wait_send()
        if a1_copy[i] is not None:
            @pl.when(has_prev)
            def _(i=i):
                a1_copy[i].wait_send()


def write(*refs):
    count = len(refs) // 3
    src, dst, (*held, sem) = refs[:count], refs[count : 2 * count], refs[2 * count :]
    inward = [pltpu.make_async_copy(a, b, sem.at[0, i]) for i, (a, b) in enumerate(zip(src, held))]
    outward = [pltpu.make_async_copy(a, b, sem.at[1, i]) for i, (a, b) in enumerate(zip(held, dst))]
    for c in inward:
        c.start()
    for a, b in zip(inward, outward):
        a.wait()
        b.start()
    for c in outward:
        c.wait()


def body(signal, cotangent, p1, w1, m1, p2, w2, m2):
    seqs, steps, c = signal.shape
    count, groups = lax.axis_size("tm"), lax.axis_size("dp")
    gate = p1.shape[1]
    scale = 1.0 / math.sqrt(seqs * groups * steps * count)
    fused = (groups, count) == (2, 16)
    chunks = ((512, 256), (0, 256), (256, 256), (768, 128), (896, 128))
    nch = len(chunks)
    hbm = pl.BlockSpec(memory_space=pltpu.HBM)
    S = jax.ShapeDtypeStruct
    dma = pltpu.SemaphoreType.DMA
    wide = (2 * gate + c) // 128 * c
    packed = S((wide, 128), BF16 if fused else F32)
    args = (signal.reshape(steps, c), cotangent.reshape(steps, c), p1, w1, m1, p2, w2, m2)
    half = wide // 2
    per_sum = [
        pltpu.VMEM((wide, 128), F32),
        pltpu.VMEM((half, 128), BF16),
        pltpu.VMEM((half, 128), BF16),
        pltpu.VMEM((3, half // 4, 128), BF16),
        pltpu.VMEM((3, half // 16, 128), BF16),
        pltpu.VMEM((half, 128), BF16),
        pltpu.VMEM((half // 4, 128), BF16),
        dma((14,)),
        dma((14,)),
    ]
    kind = packed.dtype
    shapes = [S((steps, c), BF16)] + [S((c, gate), kind), S((c, gate), kind), S((c, c), kind)] * 2
    held = [pltpu.VMEM(a.shape, a.dtype) for a in shapes]
    out = pl.pallas_call(
        functools.partial(kernel, count, SECOND_DILATION // steps, steps, chunks, scale, fused),
        out_shape=shapes,
        in_specs=[hbm] * 8,
        out_specs=[hbm] * 7,
        scratch_shapes=[pltpu.VMEM(a.shape, BF16) for a in args]
        + [
            *held,
            pltpu.VMEM(packed.shape, packed.dtype),
            pltpu.VMEM(packed.shape, packed.dtype),
            dma((7,)),
            pltpu.VMEM((FIRST_DILATION, c), BF16),
            pltpu.VMEM((steps, c), F32),
            pltpu.VMEM((steps, c), F32),
            pltpu.VMEM((steps, c), BF16),
            pltpu.VMEM((steps, c), BF16),
            pltpu.VMEM((steps, c), BF16),
            pltpu.VMEM((steps, c), BF16),
            pltpu.VMEM((steps, c), BF16),
            pltpu.VMEM((steps, gate), F32),
            pltpu.VMEM((steps, c), F32),
            pltpu.VMEM((steps, c), F32),
            pltpu.VMEM((steps, c), BF16),
            pltpu.VMEM((FIRST_DILATION, c), BF16),
            pltpu.VMEM((steps, c), F32),
            dma((8,)),
            dma, dma,
            dma((nch,)), dma((nch,)), dma((nch,)), dma((nch,)), dma((nch,)), dma((nch,)),
        ]
        + (per_sum * 2 if fused else []),
        compiler_params=pltpu.CompilerParams(
            collective_id=0, has_side_effects=True, vmem_limit_bytes=62 * 1024 * 1024
        ),
        name="layers",
    )(*args)
    if fused:
        out = pl.pallas_call(
            write,
            out_shape=shapes,
            in_specs=[hbm] * 7,
            out_specs=[hbm] * 7,
            scratch_shapes=held + [dma((2, 7))],
            compiler_params=pltpu.CompilerParams(vmem_limit_bytes=62 * 1024 * 1024),
            name="write",
        )(*out)
        grads = tuple(out[1:])
    else:
        grads = tuple((t * scale).astype(BF16) for t in lax.psum(tuple(out[1:]), ("dp", "tm")))
    return (out[0].reshape(signal.shape),) + grads


def solution(mesh):
    in_specs = (P("dp", "tm", None), P("dp", "tm", None), P(), P(), P(), P(), P(), P())
    out_specs = (P("dp", "tm", None), P(), P(), P(), P(), P(), P())
    return jax.shard_map(body, mesh=mesh, in_specs=in_specs, out_specs=out_specs, check_vma=False)
```

```python
import functools
import math

import jax
import jax.numpy as jnp
from jax import lax
from jax.experimental import pallas as pl
from jax.experimental.pallas import tpu as pltpu
from jax.sharding import PartitionSpec as P

FIRST_DILATION = 512
SECOND_DILATION = 8192
MESH = pl.DeviceIdType.MESH
F32 = jnp.float32
BF16 = jnp.bfloat16


def mm(a, b):
    return lax.dot_general(a, b, (((1,), (0,)), ((), ())), preferred_element_type=F32)


def mm_tn(a, b):
    return lax.dot_general(a, b, (((0,), (0,)), ((), ())), preferred_element_type=F32)


def sigmoid(x):
    return 0.5 * jnp.tanh(0.5 * x) + 0.5


class Sum:
    def __init__(self, acc, pack, got1, got2, got3, sum1, sum2, res, ss, rs, scale):
        self.acc, self.pack, self.got1, self.got2, self.got3 = acc, pack, got1, got2, got3
        self.sum1, self.sum2, self.res, self.ss, self.rs, self.scale = sum1, sum2, res, ss, rs, scale
        half = acc.shape[0] // 2
        quarter, piece = half // 4, half // 16
        self.half, self.quarter, self.piece = half, quarter, piece
        dp, me = lax.axis_index("dp"), lax.axis_index("tm")
        q, p, z, partner, plane, column = places(dp, me)
        self.mine = pl.multiple_of(q * half, half)
        self.other = pl.multiple_of((1 - q) * half, half)
        self.base2 = pl.multiple_of(q * half + p * quarter, quarter)
        self.base3 = pl.multiple_of(q * half + p * quarter + z * piece, piece)
        self.own2 = pl.multiple_of(p * quarter, quarter)
        self.own3 = pl.multiple_of(z * piece, piece)
        sem = iter(range(14))

        def copy(src, dst, target):
            i = next(sem)
            return pltpu.make_async_remote_copy(
                src_ref=src, dst_ref=dst, send_sem=ss.at[i], recv_sem=rs.at[i], device_id=target, device_id_type=MESH
            )

        self.c1 = [copy(pack, got1, partner)]
        self.c2 = []
        for r, (there, place) in enumerate(plane):
            rows = pl.ds(pl.multiple_of(place * quarter, quarter), quarter)
            self.c2.append(copy(sum1.at[rows], got2.at[r], there))
        self.c3 = []
        for r, (there, place) in enumerate(column):
            rows = pl.ds(pl.multiple_of(place * piece, piece), piece)
            self.c3.append(copy(sum2.at[rows], got3.at[r], there))
        three, two = res.at[pl.ds(self.base3, piece)], res.at[pl.ds(self.base2, quarter)]
        one = res.at[pl.ds(self.mine, half)]
        self.g3 = [copy(three, three, there) for there, _ in column]
        self.g2 = [copy(two, two, there) for there, _ in plane]
        self.g1 = [copy(one, one, partner)]

    def add(self, first, past, now, mix):
        for at, value in ((0, past), (4, now), (8, mix)):
            if value is None:
                continue
            for j in range(value.shape[1] // 128):
                rows = pl.ds((at + j) * value.shape[0], value.shape[0])
                part = value[:, j * 128 : (j + 1) * 128]
                self.acc[rows, :] = part if first else self.acc[rows, :] + part

    def start(self, copies):
        for c in copies:
            c.start()

    def arrive(self, copies):
        for c in copies:
            c.wait_recv()

    def send1(self):
        self.pack[...] = self.acc[pl.ds(self.other, self.half), :].astype(BF16)
        self.start(self.c1)

    def send2(self):
        self.arrive(self.c1)
        total = self.acc[pl.ds(self.mine, self.half), :] + self.got1[...].astype(F32)
        self.acc[pl.ds(self.mine, self.half), :] = total
        self.sum1[...] = total.astype(BF16)
        self.start(self.c2)

    def send3(self):
        self.arrive(self.c2)
        total = self.acc[pl.ds(self.base2, self.quarter), :]
        for r in range(3):
            total = total + self.got2[r].astype(F32)
        self.acc[pl.ds(self.base2, self.quarter), :] = total
        self.sum2[...] = total.astype(BF16)
        self.start(self.c3)

    def back3(self):
        self.arrive(self.c3)
        total = self.acc[pl.ds(self.base3, self.piece), :]
        for r in range(3):
            total = total + self.got3[r].astype(F32)
        self.res[pl.ds(self.base3, self.piece), :] = (total * self.scale).astype(BF16)
        self.start(self.g3)

    def back2(self):
        self.arrive(self.g3)
        self.start(self.g2)

    def back1(self):
        self.arrive(self.g2)
        self.start(self.g1)

    def finish(self):
        self.arrive(self.g1)

    def drain(self):
        for c in self.c1 + self.c2 + self.c3 + self.g3 + self.g2 + self.g1:
            c.wait_send()


class Local(Sum):
    def __init__(self, acc):
        self.acc = acc

    def nothing(self):
        pass

    send1 = send2 = send3 = back3 = back2 = back1 = finish = drain = nothing


def places(dp, me):
    q, x, z = lax.rem(me, 2), lax.rem(lax.div(me, 2), 2), lax.div(me, 4)
    z0, z1 = lax.rem(z, 2), lax.div(z, 2)
    partner = {"dp": dp, "tm": me + 1 - 2 * q}
    plane, column = [], []
    for r in (1, 2, 3):
        lo, hi = r % 2, r // 2
        xx = x + lo * (1 - 2 * x)
        yy = dp + hi * (1 - 2 * dp)
        plane.append(({"dp": yy, "tm": me + 2 * (xx - x)}, yy * 2 + xx))
        zz = z + lo * (1 - 2 * z0) + 2 * hi * (1 - 2 * z1)
        column.append(({"dp": dp, "tm": me + 4 * (zz - z)}, zz))
    return q, dp * 2 + x, z, partner, plane, column


def kernel(count, offset, steps, chunks, scale, fused, *refs):
    hbm, refs = refs[:8], refs[8:]
    results, refs = refs[:7], refs[7:]
    vmem, refs = refs[:8], refs[8:]
    local, out1, out2, store, refs = refs[:7], refs[7], refs[8], refs[9], refs[10:]
    gsig = local[0]
    stores = [pltpu.make_async_copy(src, dst, store.at[i]) for i, (src, dst) in enumerate(zip(local, results))]

    def unpack(packed, first):
        block = 0
        for i in range(first, first + 3):
            height, width = local[i].shape
            for j in range(width // 128):
                local[i][:, j * 128 : (j + 1) * 128] = packed[pl.ds(block * height, height), :]
                block += 1
            stores[i].start()
    halo, f1, g1, h1, mid, past2, ahead2, back2, pre2, hg2, loc2, ahead1, back1, loc1 = refs[:14]
    h2, up1, pg1, pg2, sigt, midt, h1t, halot, m2t, p2t, w2t, m1t, p1t, w1t = refs[14:28]
    refs = refs[:14] + refs[28:]
    load, halo_s, halo_r, mid_s, mid_r, a2_s, a2_r, a1_s, a1_r = refs[14:23]
    sig, cot, p1, w1, m1, p2, w2, m2 = vmem
    loads = {}
    for i, (src, dst) in enumerate(zip(hbm, vmem)):
        loads[i] = pltpu.make_async_copy(src, dst, load.at[i])
    for i in (0, 3, 2, 4, 6, 1, 7, 5):
        loads[i].start()

    d1 = FIRST_DILATION
    c = sig.shape[1]
    me = lax.axis_index("tm")
    has_prev, has_next = me > 0, me < count - 1
    has_far, has_near = me < count - offset, me >= offset
    nxt, prv = lax.rem(me + 1, count), lax.rem(me + count - 1, count)
    far, near = lax.rem(me + offset, count), lax.rem(me + count - offset, count)

    barrier = pltpu.get_barrier_semaphore()
    peers = sum(there.astype(jnp.int32) for there in (has_prev, has_next, has_far, has_near))
    for there, target in ((has_prev, prv), (has_next, nxt), (has_far, far), (has_near, near)):
        @pl.when(there)
        def _(target=target):
            pl.semaphore_signal(barrier, inc=1, device_id={"tm": target}, device_id_type=MESH)
    if fused:
        _, _, _, partner, plane, column = places(lax.axis_index("dp"), me)
        for target in [partner] + [there for there, _ in plane + column]:
            pl.semaphore_signal(barrier, inc=1, device_id=target, device_id_type=MESH)
        peers = peers + 7
    pl.semaphore_wait(barrier, peers)
    if fused:
        per = refs[23:]
        sum_one = Sum(*per[:7], out1, *per[7:9], scale)
        sum_two = Sum(*per[9:16], out2, *per[16:18], scale)
    else:
        sum_one, sum_two = Local(out1), Local(out2)

    def copy(src, dst, s, r, target):
        return pltpu.make_async_remote_copy(
            src_ref=src, dst_ref=dst, send_sem=s, recv_sem=r, device_id={"tm": target}, device_id_type=MESH
        )

    halo_copy = copy(hbm[0].at[pl.ds(steps - d1, d1)], halo, halo_s, halo_r, nxt)
    mid_copy, a2_copy, a1_copy = [], [], []
    for i, (at, size) in enumerate(chunks):
        rows = pl.ds(at, size)
        mid_copy.append(copy(mid.at[rows], past2.at[rows], mid_s.at[i], mid_r.at[i], far))
        a2_copy.append(copy(ahead2.at[rows], back2.at[rows], a2_s.at[i], a2_r.at[i], near))
        a1_copy.append(copy(ahead1.at[rows], back1.at[rows], a1_s.at[i], a1_r.at[i], prv) if at < d1 else None)

    @pl.when(has_next)
    def _():
        halo_copy.start()

    @pl.when(jnp.logical_not(has_prev))
    def _():
        halo[...] = jnp.zeros_like(halo)

    @pl.when(jnp.logical_not(has_near))
    def _():
        past2[...] = jnp.zeros_like(past2)

    @pl.when(jnp.logical_not(has_far))
    def _():
        back2[...] = jnp.zeros_like(back2)

    @pl.when(jnp.logical_not(has_next))
    def _():
        back1[...] = jnp.zeros_like(back1)

    def past1(at, size):
        return halo[pl.ds(at, size), :] if at < d1 else sig[pl.ds(at - d1, size), :]

    for i in (0, 3, 2, 4):
        loads[i].wait()
    def send_middle(i):
        @pl.when(has_far)
        def _():
            if i >= 2:
                mid_copy[i - 2].wait_send()
            mid_copy[i].start()

    waited_halo = False
    for i, (at, size) in enumerate(chunks):
        rows = pl.ds(at, size)
        if at < d1 and not waited_halo:
            waited_halo = True

            @pl.when(has_prev)
            def _():
                halo_copy.wait_recv()
        u = sig[rows, :]
        pre = mm(past1(at, size), p1[...]) + mm(u, w1[...])
        f = jnp.tanh(pre[:, :c])
        g = sigmoid(pre[:, c:])
        hid = (f * g).astype(BF16)
        f1[rows, :] = f
        g1[rows, :] = g
        h1[rows, :] = hid
        mid[rows, :] = (u.astype(F32) + mm(hid, m1[...])).astype(BF16)

        if i < 2:
            send_middle(i)

    for i in (6, 1, 7, 5):
        loads[i].wait()
    for weight, turned in ((m2, m2t), (p2, p2t), (w2, w2t), (m1, m1t), (p1, p1t), (w1, w1t)):
        turned[...] = weight[...].T
    for at, size in chunks:
        rows = pl.ds(at, size)
        pre2[rows, :] = mm(mid[rows, :], w2[...])
        hg2[rows, :] = mm(cot[rows, :], m2t[...])
    for at, size in chunks:
        rows = pl.ds(at, size)
        sigt[:, rows] = sig[rows, :].T
        midt[:, rows] = mid[rows, :].T
        h1t[:, rows] = h1[rows, :].T
        if at < d1:
            halot[:, rows] = halo[rows, :].T

    def second(i):
        at, size = chunks[i]
        rows = pl.ds(at, size)

        @pl.when(has_near)
        def _():
            mid_copy[i].wait_recv()
        up = cot[rows, :]
        pre = mm(past2[rows, :], p2[...]) + pre2[rows, :]
        f = jnp.tanh(pre[:, :c])
        g = sigmoid(pre[:, c:])
        h2[rows, :] = (f * g).astype(BF16)
        hg = hg2[rows, :]
        pg = jnp.concatenate([hg * g * (1.0 - f * f), hg * f * g * (1.0 - g)], axis=1).astype(BF16)
        pg2[rows, :] = pg

        @pl.when(has_near)
        def _():
            ahead2[rows, :] = mm(pg, p2t[...]).astype(BF16)
            a2_copy[i].start()
        loc2[rows, :] = up.astype(F32) + mm(pg, w2t[...])

    def second_terms(at, size, begin):
        rows = pl.ds(at, size)
        pg = pg2[rows, :]
        sum_two.add(begin, None, mm(midt[:, rows], pg), mm_tn(h2[rows, :], cot[rows, :]))
        if begin:
            sum_two.acc[pl.ds(0, 4 * c), :] = jnp.zeros((4 * c, 128), F32)

        @pl.when(has_near)
        def _():
            sum_two.add(False, mm_tn(past2[rows, :], pg), None, None)

    def first(i):
        at, size = chunks[i]
        rows = pl.ds(at, size)

        @pl.when(has_far)
        def _():
            a2_copy[i].wait_recv()
        up = (loc2[rows, :] + back2[rows, :].astype(F32)).astype(BF16)
        up1[rows, :] = up
        hg = mm(up, m1t[...])
        f, g = f1[rows, :], g1[rows, :]
        pg = jnp.concatenate([hg * g * (1.0 - f * f), hg * f * g * (1.0 - g)], axis=1).astype(BF16)
        pg1[rows, :] = pg

    def first_grads(i):
        at, size = chunks[i]
        rows = pl.ds(at, size)
        pg = pg1[rows, :]
        ahead1[rows, :] = mm(pg, p1t[...]).astype(BF16)
        if at < d1:
            @pl.when(has_prev)
            def _():
                a1_copy[i].start()
        loc1[rows, :] = up1[rows, :].astype(F32) + mm(pg, w1t[...])

    def first_terms(at, size, begin):
        rows = pl.ds(at, size)
        past = halot[:, rows] if at < d1 else sigt[:, pl.ds(at - d1, size)]
        pg = pg1[rows, :]
        sum_one.add(begin, mm(past, pg), mm(sigt[:, rows], pg), mm(h1t[:, rows], up1[rows, :]))

    span = chunks[1][1]
    second(0)
    send_middle(2)
    second(1)
    send_middle(3)
    second_terms(d1, span, True)
    first(0)
    first_grads(0)
    second(2)
    second_terms(0, d1, False)
    first(1)
    first_grads(1)
    second(3)
    second_terms(d1 + span, span, False)
    sum_two.send1()
    first_terms(d1, span, True)
    first(2)
    first_grads(2)
    sum_two.send2()
    first_terms(0, d1, False)
    sum_two.send3()
    first(3)
    first_terms(d1 + span, span, False)
    sum_one.send1()
    sum_two.back3()
    first_grads(3)
    sum_one.send2()
    sum_two.back2()

    for i, (at, size) in enumerate(chunks):
        if at < d1:
            @pl.when(has_next)
            def _(i=i):
                a1_copy[i].wait_recv()
    rest = steps - d1
    if rest:
        gsig[pl.ds(0, rest), :] = (loc1[pl.ds(0, rest), :] + ahead1[pl.ds(d1, rest), :].astype(F32)).astype(BF16)
    gsig[pl.ds(rest, d1), :] = (loc1[pl.ds(rest, d1), :] + back1[...].astype(F32)).astype(BF16)
    stores[0].start()

    sum_one.send3()
    sum_two.back1()
    sum_one.back3()
    sum_one.back2()
    sum_two.finish()
    unpack(out2, 4)
    sum_one.back1()
    sum_one.finish()
    unpack(out1, 1)
    sum_one.drain()
    sum_two.drain()

    for c in stores:
        c.wait()

    @pl.when(has_next)
    def _():
        halo_copy.wait_send()
    for i in range(len(chunks)):
        if i >= len(chunks) - 2:
            @pl.when(has_far)
            def _(i=i):
                mid_copy[i].wait_send()

        @pl.when(has_near)
        def _(i=i):
            a2_copy[i].wait_send()
        if a1_copy[i] is not None:
            @pl.when(has_prev)
            def _(i=i):
                a1_copy[i].wait_send()


def write(*refs):
    count = len(refs) // 3
    src, dst, (*held, sem) = refs[:count], refs[count : 2 * count], refs[2 * count :]
    inward = [pltpu.make_async_copy(a, b, sem.at[0, i]) for i, (a, b) in enumerate(zip(src, held))]
    outward = [pltpu.make_async_copy(a, b, sem.at[1, i]) for i, (a, b) in enumerate(zip(held, dst))]
    for c in inward:
        c.start()
    for a, b in zip(inward, outward):
        a.wait()
        b.start()
    for c in outward:
        c.wait()


def body(signal, cotangent, p1, w1, m1, p2, w2, m2):
    seqs, steps, c = signal.shape
    count, groups = lax.axis_size("tm"), lax.axis_size("dp")
    gate = p1.shape[1]
    scale = 1.0 / math.sqrt(seqs * groups * steps * count)
    fused = (groups, count) == (2, 16)
    chunks = ((512, 256), (0, 256), (256, 256), (768, 256))
    nch = len(chunks)
    hbm = pl.BlockSpec(memory_space=pltpu.HBM)
    S = jax.ShapeDtypeStruct
    dma = pltpu.SemaphoreType.DMA
    wide = (2 * gate + c) // 128 * c
    packed = S((wide, 128), BF16 if fused else F32)
    args = (signal.reshape(steps, c), cotangent.reshape(steps, c), p1, w1, m1, p2, w2, m2)
    half = wide // 2
    per_sum = [
        pltpu.VMEM((wide, 128), F32),
        pltpu.VMEM((half, 128), BF16),
        pltpu.VMEM((half, 128), BF16),
        pltpu.VMEM((3, half // 4, 128), BF16),
        pltpu.VMEM((3, half // 16, 128), BF16),
        pltpu.VMEM((half, 128), BF16),
        pltpu.VMEM((half // 4, 128), BF16),
        dma((14,)),
        dma((14,)),
    ]
    kind = packed.dtype
    shapes = [S((steps, c), BF16)] + [S((c, gate), kind), S((c, gate), kind), S((c, c), kind)] * 2
    held = [pltpu.VMEM(a.shape, a.dtype) for a in shapes]
    out = pl.pallas_call(
        functools.partial(kernel, count, SECOND_DILATION // steps, steps, chunks, scale, fused),
        out_shape=shapes,
        in_specs=[hbm] * 8,
        out_specs=[hbm] * 7,
        scratch_shapes=[pltpu.VMEM(a.shape, BF16) for a in args]
        + [
            *held,
            pltpu.VMEM(packed.shape, packed.dtype),
            pltpu.VMEM(packed.shape, packed.dtype),
            dma((7,)),
            pltpu.VMEM((FIRST_DILATION, c), BF16),
            pltpu.VMEM((steps, c), F32),
            pltpu.VMEM((steps, c), F32),
            pltpu.VMEM((steps, c), BF16),
            pltpu.VMEM((steps, c), BF16),
            pltpu.VMEM((steps, c), BF16),
            pltpu.VMEM((steps, c), BF16),
            pltpu.VMEM((steps, c), BF16),
            pltpu.VMEM((steps, gate), F32),
            pltpu.VMEM((steps, c), F32),
            pltpu.VMEM((steps, c), F32),
            pltpu.VMEM((steps, c), BF16),
            pltpu.VMEM((FIRST_DILATION, c), BF16),
            pltpu.VMEM((steps, c), F32),
            pltpu.VMEM((steps, c), BF16),
            pltpu.VMEM((steps, c), BF16),
            pltpu.VMEM((steps, gate), BF16),
            pltpu.VMEM((steps, gate), BF16),
            pltpu.VMEM((c, steps), BF16),
            pltpu.VMEM((c, steps), BF16),
            pltpu.VMEM((c, steps), BF16),
            pltpu.VMEM((c, FIRST_DILATION), BF16),
            *[pltpu.VMEM((n, c), BF16) for n in (c, gate, gate, c, gate, gate)],
            dma((8,)),
            dma, dma,
            dma((nch,)), dma((nch,)), dma((nch,)), dma((nch,)), dma((nch,)), dma((nch,)),
        ]
        + (per_sum * 2 if fused else []),
        compiler_params=pltpu.CompilerParams(
            collective_id=0, has_side_effects=True, vmem_limit_bytes=62 * 1024 * 1024
        ),
        name="layers",
    )(*args)
    if fused:
        out = pl.pallas_call(
            write,
            out_shape=shapes,
            in_specs=[hbm] * 7,
            out_specs=[hbm] * 7,
            scratch_shapes=held + [dma((2, 7))],
            compiler_params=pltpu.CompilerParams(vmem_limit_bytes=62 * 1024 * 1024),
            name="write",
        )(*out)
        grads = tuple(out[1:])
    else:
        grads = tuple((t * scale).astype(BF16) for t in lax.psum(tuple(out[1:]), ("dp", "tm")))
    return (out[0].reshape(signal.shape),) + grads


def solution(mesh):
    in_specs = (P("dp", "tm", None), P("dp", "tm", None), P(), P(), P(), P(), P(), P())
    out_specs = (P("dp", "tm", None), P(), P(), P(), P(), P(), P())
    return jax.shard_map(body, mesh=mesh, in_specs=in_specs, out_specs=out_specs, check_vma=False)
```

```python
import functools
import math

import jax
import jax.numpy as jnp
from jax import lax
from jax.experimental import pallas as pl
from jax.experimental.pallas import tpu as pltpu
from jax.sharding import PartitionSpec as P

FIRST_DILATION = 512
SECOND_DILATION = 8192
MESH = pl.DeviceIdType.MESH
F32 = jnp.float32
BF16 = jnp.bfloat16


def mm(a, b):
    return lax.dot_general(a, b, (((1,), (0,)), ((), ())), preferred_element_type=F32)


def mm_nt(a, b):
    return lax.dot_general(a, b, (((1,), (1,)), ((), ())), preferred_element_type=F32)


def mm_tn(a, b):
    return lax.dot_general(a, b, (((0,), (0,)), ((), ())), preferred_element_type=F32)


def sigmoid(x):
    return 0.5 * jnp.tanh(0.5 * x) + 0.5


class Sum:
    def __init__(self, acc, pack, got1, got2, got3, sum1, sum2, res, ss, rs, scale):
        self.acc, self.pack, self.got1, self.got2, self.got3 = acc, pack, got1, got2, got3
        self.sum1, self.sum2, self.res, self.ss, self.rs, self.scale = sum1, sum2, res, ss, rs, scale
        half = acc.shape[0] // 2
        quarter, piece = half // 4, half // 16
        self.half, self.quarter, self.piece = half, quarter, piece
        dp, me = lax.axis_index("dp"), lax.axis_index("tm")
        q, p, z, partner, plane, column = places(dp, me)
        self.mine = pl.multiple_of(q * half, half)
        self.other = pl.multiple_of((1 - q) * half, half)
        self.base2 = pl.multiple_of(q * half + p * quarter, quarter)
        self.base3 = pl.multiple_of(q * half + p * quarter + z * piece, piece)
        self.own2 = pl.multiple_of(p * quarter, quarter)
        self.own3 = pl.multiple_of(z * piece, piece)
        sem = iter(range(14))

        def copy(src, dst, target):
            i = next(sem)
            return pltpu.make_async_remote_copy(
                src_ref=src, dst_ref=dst, send_sem=ss.at[i], recv_sem=rs.at[i], device_id=target, device_id_type=MESH
            )

        self.c1 = [copy(pack, got1, partner)]
        self.c2 = []
        for r, (there, place) in enumerate(plane):
            rows = pl.ds(pl.multiple_of(place * quarter, quarter), quarter)
            self.c2.append(copy(sum1.at[rows], got2.at[r], there))
        self.c3 = []
        for r, (there, place) in enumerate(column):
            rows = pl.ds(pl.multiple_of(place * piece, piece), piece)
            self.c3.append(copy(sum2.at[rows], got3.at[r], there))
        three, two = res.at[pl.ds(self.base3, piece)], res.at[pl.ds(self.base2, quarter)]
        one = res.at[pl.ds(self.mine, half)]
        self.g3 = [copy(three, three, there) for there, _ in column]
        self.g2 = [copy(two, two, there) for there, _ in plane]
        self.g1 = [copy(one, one, partner)]

    def add(self, first, past, now, mix):
        for at, value in ((0, past), (4, now), (8, mix)):
            if value is None:
                continue
            for j in range(value.shape[1] // 128):
                rows = pl.ds((at + j) * value.shape[0], value.shape[0])
                part = value[:, j * 128 : (j + 1) * 128]
                self.acc[rows, :] = part if first else self.acc[rows, :] + part

    def start(self, copies):
        for c in copies:
            c.start()

    def arrive(self, copies):
        for c in copies:
            c.wait_recv()

    def send1(self):
        self.pack[...] = self.acc[pl.ds(self.other, self.half), :].astype(BF16)
        self.start(self.c1)

    def send2(self):
        self.arrive(self.c1)
        total = self.acc[pl.ds(self.mine, self.half), :] + self.got1[...].astype(F32)
        self.acc[pl.ds(self.mine, self.half), :] = total
        self.sum1[...] = total.astype(BF16)
        self.start(self.c2)

    def send3(self):
        self.arrive(self.c2)
        total = self.acc[pl.ds(self.base2, self.quarter), :]
        for r in range(3):
            total = total + self.got2[r].astype(F32)
        self.acc[pl.ds(self.base2, self.quarter), :] = total
        self.sum2[...] = total.astype(BF16)
        self.start(self.c3)

    def back3(self):
        self.arrive(self.c3)
        total = self.acc[pl.ds(self.base3, self.piece), :]
        for r in range(3):
            total = total + self.got3[r].astype(F32)
        self.res[pl.ds(self.base3, self.piece), :] = (total * self.scale).astype(BF16)
        self.start(self.g3)

    def back2(self):
        self.arrive(self.g3)
        self.start(self.g2)

    def back1(self):
        self.arrive(self.g2)
        self.start(self.g1)

    def finish(self):
        self.arrive(self.g1)

    def drain(self):
        for c in self.c1 + self.c2 + self.c3 + self.g3 + self.g2 + self.g1:
            c.wait_send()


class Local(Sum):
    def __init__(self, acc):
        self.acc = acc

    def nothing(self):
        pass

    send1 = send2 = send3 = back3 = back2 = back1 = finish = drain = nothing


def places(dp, me):
    q, x, z = lax.rem(me, 2), lax.rem(lax.div(me, 2), 2), lax.div(me, 4)
    z0, z1 = lax.rem(z, 2), lax.div(z, 2)
    partner = {"dp": dp, "tm": me + 1 - 2 * q}
    plane, column = [], []
    for r in (1, 2, 3):
        lo, hi = r % 2, r // 2
        xx = x + lo * (1 - 2 * x)
        yy = dp + hi * (1 - 2 * dp)
        plane.append(({"dp": yy, "tm": me + 2 * (xx - x)}, yy * 2 + xx))
        zz = z + lo * (1 - 2 * z0) + 2 * hi * (1 - 2 * z1)
        column.append(({"dp": dp, "tm": me + 4 * (zz - z)}, zz))
    return q, dp * 2 + x, z, partner, plane, column


def kernel(count, offset, steps, chunks, scale, fused, *refs):
    hbm, refs = refs[:8], refs[8:]
    results, refs = refs[:7], refs[7:]
    vmem, refs = refs[:8], refs[8:]
    local, out1, out2, store, refs = refs[:7], refs[7], refs[8], refs[9], refs[10:]
    gsig = local[0]
    stores = [pltpu.make_async_copy(src, dst, store.at[i]) for i, (src, dst) in enumerate(zip(local, results))]

    def unpack(packed, first):
        block = 0
        for i in range(first, first + 3):
            height, width = local[i].shape
            for j in range(width // 128):
                local[i][:, j * 128 : (j + 1) * 128] = packed[pl.ds(block * height, height), :]
                block += 1
            stores[i].start()
    halo, f1, g1, h1, mid, past2, ahead2, back2, pre2, hg2, loc2, ahead1, back1, loc1 = refs[:14]
    h2, up1, pg1, pg2 = refs[14:18]
    refs = refs[:14] + refs[18:]
    load, halo_s, halo_r, mid_s, mid_r, a2_s, a2_r, a1_s, a1_r = refs[14:23]
    sig, cot, p1, w1, m1, p2, w2, m2 = vmem
    loads = {}
    for i, (src, dst) in enumerate(zip(hbm, vmem)):
        loads[i] = pltpu.make_async_copy(src, dst, load.at[i])
    for i in (0, 3, 2, 4, 6, 1, 7, 5):
        loads[i].start()

    d1 = FIRST_DILATION
    c = sig.shape[1]
    me = lax.axis_index("tm")
    has_prev, has_next = me > 0, me < count - 1
    has_far, has_near = me < count - offset, me >= offset
    nxt, prv = lax.rem(me + 1, count), lax.rem(me + count - 1, count)
    far, near = lax.rem(me + offset, count), lax.rem(me + count - offset, count)

    barrier = pltpu.get_barrier_semaphore()
    peers = sum(there.astype(jnp.int32) for there in (has_prev, has_next, has_far, has_near))
    for there, target in ((has_prev, prv), (has_next, nxt), (has_far, far), (has_near, near)):
        @pl.when(there)
        def _(target=target):
            pl.semaphore_signal(barrier, inc=1, device_id={"tm": target}, device_id_type=MESH)
    if fused:
        _, _, _, partner, plane, column = places(lax.axis_index("dp"), me)
        for target in [partner] + [there for there, _ in plane + column]:
            pl.semaphore_signal(barrier, inc=1, device_id=target, device_id_type=MESH)
        peers = peers + 7
    pl.semaphore_wait(barrier, peers)
    if fused:
        per = refs[23:]
        sum_one = Sum(*per[:7], out1, *per[7:9], scale)
        sum_two = Sum(*per[9:16], out2, *per[16:18], scale)
    else:
        sum_one, sum_two = Local(out1), Local(out2)

    def copy(src, dst, s, r, target):
        return pltpu.make_async_remote_copy(
            src_ref=src, dst_ref=dst, send_sem=s, recv_sem=r, device_id={"tm": target}, device_id_type=MESH
        )

    halo_copy = copy(hbm[0].at[pl.ds(steps - d1, d1)], halo, halo_s, halo_r, nxt)
    mid_copy, a2_copy, a1_copy = [], [], []
    for i, (at, size) in enumerate(chunks):
        rows = pl.ds(at, size)
        mid_copy.append(copy(mid.at[rows], past2.at[rows], mid_s.at[i], mid_r.at[i], far))
        a2_copy.append(copy(ahead2.at[rows], back2.at[rows], a2_s.at[i], a2_r.at[i], near))
        a1_copy.append(copy(ahead1.at[rows], back1.at[rows], a1_s.at[i], a1_r.at[i], prv) if at < d1 else None)

    @pl.when(has_next)
    def _():
        halo_copy.start()

    @pl.when(jnp.logical_not(has_prev))
    def _():
        halo[...] = jnp.zeros_like(halo)

    @pl.when(jnp.logical_not(has_near))
    def _():
        past2[...] = jnp.zeros_like(past2)

    @pl.when(jnp.logical_not(has_far))
    def _():
        back2[...] = jnp.zeros_like(back2)

    @pl.when(jnp.logical_not(has_next))
    def _():
        back1[...] = jnp.zeros_like(back1)

    def past1(at, size):
        return halo[pl.ds(at, size), :] if at < d1 else sig[pl.ds(at - d1, size), :]

    for i in (0, 3, 2, 4):
        loads[i].wait()
    def send_middle(i):
        @pl.when(has_far)
        def _():
            if i >= 2:
                mid_copy[i - 2].wait_send()
            mid_copy[i].start()

    waited_halo = False
    for i, (at, size) in enumerate(chunks):
        rows = pl.ds(at, size)
        if at < d1 and not waited_halo:
            waited_halo = True

            @pl.when(has_prev)
            def _():
                halo_copy.wait_recv()
        u = sig[rows, :]
        pre = mm(past1(at, size), p1[...]) + mm(u, w1[...])
        f = jnp.tanh(pre[:, :c])
        g = sigmoid(pre[:, c:])
        hid = (f * g).astype(BF16)
        f1[rows, :] = f
        g1[rows, :] = g
        h1[rows, :] = hid
        mid[rows, :] = (u.astype(F32) + mm(hid, m1[...])).astype(BF16)

        if i < 2:
            send_middle(i)

    for i in (6, 1, 7, 5):
        loads[i].wait()
    for at, size in chunks:
        rows = pl.ds(at, size)
        pre2[rows, :] = mm(mid[rows, :], w2[...])
        hg2[rows, :] = mm_nt(cot[rows, :], m2[...])
    def second(i):
        at, size = chunks[i]
        rows = pl.ds(at, size)

        @pl.when(has_near)
        def _():
            mid_copy[i].wait_recv()
        up = cot[rows, :]
        pre = mm(past2[rows, :], p2[...]) + pre2[rows, :]
        f = jnp.tanh(pre[:, :c])
        g = sigmoid(pre[:, c:])
        h2[rows, :] = (f * g).astype(BF16)
        hg = hg2[rows, :]
        pg = jnp.concatenate([hg * g * (1.0 - f * f), hg * f * g * (1.0 - g)], axis=1).astype(BF16)
        pg2[rows, :] = pg

        @pl.when(has_near)
        def _():
            ahead2[rows, :] = mm_nt(pg, p2[...]).astype(BF16)
            a2_copy[i].start()
        loc2[rows, :] = up.astype(F32) + mm_nt(pg, w2[...])

    def second_terms(at, size, begin):
        rows = pl.ds(at, size)
        pg = pg2[rows, :]
        sum_two.add(begin, None, mm_tn(mid[rows, :], pg), mm_tn(h2[rows, :], cot[rows, :]))
        if begin:
            sum_two.acc[pl.ds(0, 4 * c), :] = jnp.zeros((4 * c, 128), F32)

        @pl.when(has_near)
        def _():
            sum_two.add(False, mm_tn(past2[rows, :], pg), None, None)

    def first(i):
        at, size = chunks[i]
        rows = pl.ds(at, size)

        @pl.when(has_far)
        def _():
            a2_copy[i].wait_recv()
        up = (loc2[rows, :] + back2[rows, :].astype(F32)).astype(BF16)
        up1[rows, :] = up
        hg = mm_nt(up, m1[...])
        f, g = f1[rows, :], g1[rows, :]
        pg = jnp.concatenate([hg * g * (1.0 - f * f), hg * f * g * (1.0 - g)], axis=1).astype(BF16)
        pg1[rows, :] = pg

    def first_grads(i):
        at, size = chunks[i]
        rows = pl.ds(at, size)
        pg = pg1[rows, :]
        ahead1[rows, :] = mm_nt(pg, p1[...]).astype(BF16)
        if at < d1:
            @pl.when(has_prev)
            def _():
                a1_copy[i].start()
        loc1[rows, :] = up1[rows, :].astype(F32) + mm_nt(pg, w1[...])

    def first_terms(at, size, begin):
        rows = pl.ds(at, size)
        pg = pg1[rows, :]
        sum_one.add(begin, mm_tn(past1(at, size), pg), mm_tn(sig[rows, :], pg), mm_tn(h1[rows, :], up1[rows, :]))

    span = chunks[1][1]
    second(0)
    send_middle(2)
    second(1)
    send_middle(3)
    first(0)
    first_grads(0)
    second(2)
    second_terms(d1, span, True)
    first(1)
    first_grads(1)
    second(3)
    second_terms(0, d1, False)
    second_terms(d1 + span, span, False)
    sum_two.send1()
    first_terms(d1, span, True)
    first(2)
    sum_two.send2()
    first_grads(2)
    first_terms(0, d1, False)
    first(3)
    first_terms(d1 + span, span, False)
    sum_one.send1()
    sum_two.send3()
    first_grads(3)
    sum_one.send2()
    sum_two.back3()
    sum_two.back2()

    for i, (at, size) in enumerate(chunks):
        if at < d1:
            @pl.when(has_next)
            def _(i=i):
                a1_copy[i].wait_recv()
    rest = steps - d1
    if rest:
        gsig[pl.ds(0, rest), :] = (loc1[pl.ds(0, rest), :] + ahead1[pl.ds(d1, rest), :].astype(F32)).astype(BF16)
    gsig[pl.ds(rest, d1), :] = (loc1[pl.ds(rest, d1), :] + back1[...].astype(F32)).astype(BF16)
    stores[0].start()

    sum_one.send3()
    sum_two.back1()
    sum_one.back3()
    sum_one.back2()
    sum_two.finish()
    unpack(out2, 4)
    sum_one.back1()
    sum_one.finish()
    unpack(out1, 1)
    sum_one.drain()
    sum_two.drain()

    for c in stores:
        c.wait()

    @pl.when(has_next)
    def _():
        halo_copy.wait_send()
    for i in range(len(chunks)):
        if i >= len(chunks) - 2:
            @pl.when(has_far)
            def _(i=i):
                mid_copy[i].wait_send()

        @pl.when(has_near)
        def _(i=i):
            a2_copy[i].wait_send()
        if a1_copy[i] is not None:
            @pl.when(has_prev)
            def _(i=i):
                a1_copy[i].wait_send()


def write(*refs):
    count = len(refs) // 3
    src, dst, (*held, sem) = refs[:count], refs[count : 2 * count], refs[2 * count :]
    inward = [pltpu.make_async_copy(a, b, sem.at[0, i]) for i, (a, b) in enumerate(zip(src, held))]
    outward = [pltpu.make_async_copy(a, b, sem.at[1, i]) for i, (a, b) in enumerate(zip(held, dst))]
    for c in inward:
        c.start()
    for a, b in zip(inward, outward):
        a.wait()
        b.start()
    for c in outward:
        c.wait()


def body(signal, cotangent, p1, w1, m1, p2, w2, m2):
    seqs, steps, c = signal.shape
    count, groups = lax.axis_size("tm"), lax.axis_size("dp")
    gate = p1.shape[1]
    scale = 1.0 / math.sqrt(seqs * groups * steps * count)
    fused = (groups, count) == (2, 16)
    chunks = ((512, 256), (0, 256), (256, 256), (768, 256))
    nch = len(chunks)
    hbm = pl.BlockSpec(memory_space=pltpu.HBM)
    S = jax.ShapeDtypeStruct
    dma = pltpu.SemaphoreType.DMA
    wide = (2 * gate + c) // 128 * c
    packed = S((wide, 128), BF16 if fused else F32)
    args = (signal.reshape(steps, c), cotangent.reshape(steps, c), p1, w1, m1, p2, w2, m2)
    half = wide // 2
    per_sum = [
        pltpu.VMEM((wide, 128), F32),
        pltpu.VMEM((half, 128), BF16),
        pltpu.VMEM((half, 128), BF16),
        pltpu.VMEM((3, half // 4, 128), BF16),
        pltpu.VMEM((3, half // 16, 128), BF16),
        pltpu.VMEM((half, 128), BF16),
        pltpu.VMEM((half // 4, 128), BF16),
        dma((14,)),
        dma((14,)),
    ]
    kind = packed.dtype
    shapes = [S((steps, c), BF16)] + [S((c, gate), kind), S((c, gate), kind), S((c, c), kind)] * 2
    held = [pltpu.VMEM(a.shape, a.dtype) for a in shapes]
    out = pl.pallas_call(
        functools.partial(kernel, count, SECOND_DILATION // steps, steps, chunks, scale, fused),
        out_shape=shapes,
        in_specs=[hbm] * 8,
        out_specs=[hbm] * 7,
        scratch_shapes=[pltpu.VMEM(a.shape, BF16) for a in args]
        + [
            *held,
            pltpu.VMEM(packed.shape, packed.dtype),
            pltpu.VMEM(packed.shape, packed.dtype),
            dma((7,)),
            pltpu.VMEM((FIRST_DILATION, c), BF16),
            pltpu.VMEM((steps, c), F32),
            pltpu.VMEM((steps, c), F32),
            pltpu.VMEM((steps, c), BF16),
            pltpu.VMEM((steps, c), BF16),
            pltpu.VMEM((steps, c), BF16),
            pltpu.VMEM((steps, c), BF16),
            pltpu.VMEM((steps, c), BF16),
            pltpu.VMEM((steps, gate), F32),
            pltpu.VMEM((steps, c), F32),
            pltpu.VMEM((steps, c), F32),
            pltpu.VMEM((steps, c), BF16),
            pltpu.VMEM((FIRST_DILATION, c), BF16),
            pltpu.VMEM((steps, c), F32),
            pltpu.VMEM((steps, c), BF16),
            pltpu.VMEM((steps, c), BF16),
            pltpu.VMEM((steps, gate), BF16),
            pltpu.VMEM((steps, gate), BF16),
            dma((8,)),
            dma, dma,
            dma((nch,)), dma((nch,)), dma((nch,)), dma((nch,)), dma((nch,)), dma((nch,)),
        ]
        + (per_sum * 2 if fused else []),
        compiler_params=pltpu.CompilerParams(
            collective_id=0, has_side_effects=True, vmem_limit_bytes=62 * 1024 * 1024
        ),
        name="layers",
    )(*args)
    if fused:
        out = pl.pallas_call(
            write,
            out_shape=shapes,
            in_specs=[hbm] * 7,
            out_specs=[hbm] * 7,
            scratch_shapes=held + [dma((2, 7))],
            compiler_params=pltpu.CompilerParams(vmem_limit_bytes=62 * 1024 * 1024),
            name="write",
        )(*out)
        grads = tuple(out[1:])
    else:
        grads = tuple((t * scale).astype(BF16) for t in lax.psum(tuple(out[1:]), ("dp", "tm")))
    return (out[0].reshape(signal.shape),) + grads


def solution(mesh):
    in_specs = (P("dp", "tm", None), P("dp", "tm", None), P(), P(), P(), P(), P(), P())
    out_specs = (P("dp", "tm", None), P(), P(), P(), P(), P(), P())
    return jax.shard_map(body, mesh=mesh, in_specs=in_specs, out_specs=out_specs, check_vma=False)
```

```python
import functools
import math

import jax
import jax.numpy as jnp
from jax import lax
from jax.experimental import pallas as pl
from jax.experimental.pallas import tpu as pltpu
from jax.sharding import PartitionSpec as P

FIRST_DILATION = 512
SECOND_DILATION = 8192
MESH = pl.DeviceIdType.MESH
F32 = jnp.float32
BF16 = jnp.bfloat16


def mm(a, b):
    return lax.dot_general(a, b, (((1,), (0,)), ((), ())), preferred_element_type=F32)


def mm_nt(a, b):
    return lax.dot_general(a, b, (((1,), (1,)), ((), ())), preferred_element_type=F32)


def mm_tn(a, b):
    return lax.dot_general(a, b, (((0,), (0,)), ((), ())), preferred_element_type=F32)


def sigmoid(x):
    return 0.5 * jnp.tanh(0.5 * x) + 0.5


class Sum:
    def __init__(self, acc, pack, got1, got2, got3, sum1, sum2, res, ss, rs, scale):
        self.acc, self.pack, self.got1, self.got2, self.got3 = acc, pack, got1, got2, got3
        self.sum1, self.sum2, self.res, self.ss, self.rs, self.scale = sum1, sum2, res, ss, rs, scale
        half = acc.shape[0] // 2
        quarter, piece = half // 4, half // 16
        self.half, self.quarter, self.piece = half, quarter, piece
        dp, me = lax.axis_index("dp"), lax.axis_index("tm")
        q, p, z, partner, plane, column = places(dp, me)
        self.mine = pl.multiple_of(q * half, half)
        self.other = pl.multiple_of((1 - q) * half, half)
        self.base2 = pl.multiple_of(q * half + p * quarter, quarter)
        self.base3 = pl.multiple_of(q * half + p * quarter + z * piece, piece)
        self.own2 = pl.multiple_of(p * quarter, quarter)
        self.own3 = pl.multiple_of(z * piece, piece)
        sem = iter(range(14))

        def copy(src, dst, target):
            i = next(sem)
            return pltpu.make_async_remote_copy(
                src_ref=src, dst_ref=dst, send_sem=ss.at[i], recv_sem=rs.at[i], device_id=target, device_id_type=MESH
            )

        self.c1 = [copy(pack, got1, partner)]
        self.c2 = []
        for r, (there, place) in enumerate(plane):
            rows = pl.ds(pl.multiple_of(place * quarter, quarter), quarter)
            self.c2.append(copy(sum1.at[rows], got2.at[r], there))
        self.c3 = []
        for r, (there, place) in enumerate(column):
            rows = pl.ds(pl.multiple_of(place * piece, piece), piece)
            self.c3.append(copy(sum2.at[rows], got3.at[r], there))
        three, two = res.at[pl.ds(self.base3, piece)], res.at[pl.ds(self.base2, quarter)]
        one = res.at[pl.ds(self.mine, half)]
        self.g3 = [copy(three, three, there) for there, _ in column]
        self.g2 = [copy(two, two, there) for there, _ in plane]
        self.g1 = [copy(one, one, partner)]

    def add(self, first, past, now, mix):
        for at, value in ((0, past), (4, now), (8, mix)):
            if value is None:
                continue
            for j in range(value.shape[1] // 128):
                rows = pl.ds((at + j) * value.shape[0], value.shape[0])
                part = value[:, j * 128 : (j + 1) * 128]
                self.acc[rows, :] = part if first else self.acc[rows, :] + part

    def start(self, copies):
        for c in copies:
            c.start()

    def arrive(self, copies):
        for c in copies:
            c.wait_recv()

    def send1(self):
        self.pack[...] = self.acc[pl.ds(self.other, self.half), :].astype(BF16)
        self.start(self.c1)

    def send2(self):
        self.arrive(self.c1)
        total = self.acc[pl.ds(self.mine, self.half), :] + self.got1[...].astype(F32)
        self.acc[pl.ds(self.mine, self.half), :] = total
        self.sum1[...] = total.astype(BF16)
        self.start(self.c2)

    def send3(self):
        self.arrive(self.c2)
        total = self.acc[pl.ds(self.base2, self.quarter), :]
        for r in range(3):
            total = total + self.got2[r].astype(F32)
        self.acc[pl.ds(self.base2, self.quarter), :] = total
        self.sum2[...] = total.astype(BF16)
        self.start(self.c3)

    def back3(self):
        self.arrive(self.c3)
        total = self.acc[pl.ds(self.base3, self.piece), :]
        for r in range(3):
            total = total + self.got3[r].astype(F32)
        self.res[pl.ds(self.base3, self.piece), :] = (total * self.scale).astype(BF16)
        self.start(self.g3)

    def back2(self):
        self.arrive(self.g3)
        self.start(self.g2)

    def back1(self):
        self.arrive(self.g2)
        self.start(self.g1)

    def finish(self):
        self.arrive(self.g1)

    def drain(self):
        for c in self.c1 + self.c2 + self.c3 + self.g3 + self.g2 + self.g1:
            c.wait_send()


class Local(Sum):
    def __init__(self, acc):
        self.acc = acc

    def nothing(self):
        pass

    send1 = send2 = send3 = back3 = back2 = back1 = finish = drain = nothing


def places(dp, me):
    q, x, z = lax.rem(me, 2), lax.rem(lax.div(me, 2), 2), lax.div(me, 4)
    z0, z1 = lax.rem(z, 2), lax.div(z, 2)
    partner = {"dp": dp, "tm": me + 1 - 2 * q}
    plane, column = [], []
    for r in (1, 2, 3):
        lo, hi = r % 2, r // 2
        xx = x + lo * (1 - 2 * x)
        yy = dp + hi * (1 - 2 * dp)
        plane.append(({"dp": yy, "tm": me + 2 * (xx - x)}, yy * 2 + xx))
        zz = z + lo * (1 - 2 * z0) + 2 * hi * (1 - 2 * z1)
        column.append(({"dp": dp, "tm": me + 4 * (zz - z)}, zz))
    return q, dp * 2 + x, z, partner, plane, column


def kernel(count, offset, steps, chunks, scale, fused, *refs):
    hbm, refs = refs[:8], refs[8:]
    results, refs = refs[:7], refs[7:]
    vmem, refs = refs[:8], refs[8:]
    local, out1, out2, store, refs = refs[:7], refs[7], refs[8], refs[9], refs[10:]
    gsig = local[0]
    stores = [pltpu.make_async_copy(src, dst, store.at[i]) for i, (src, dst) in enumerate(zip(local, results))]

    def unpack(packed, first):
        block = 0
        for i in range(first, first + 3):
            height, width = local[i].shape
            for j in range(width // 128):
                local[i][:, j * 128 : (j + 1) * 128] = packed[pl.ds(block * height, height), :]
                block += 1
            stores[i].start()
    halo, f1, g1, h1, mid, past2, ahead2, back2, pre2, hg2, loc2, ahead1, back1, loc1 = refs[:14]
    h2, up1, pg1, pg2 = refs[14:18]
    refs = refs[:14] + refs[18:]
    load, halo_s, halo_r, mid_s, mid_r, a2_s, a2_r, a1_s, a1_r = refs[14:23]
    sig, cot, p1, w1, m1, p2, w2, m2 = vmem
    loads = {}
    for i, (src, dst) in enumerate(zip(hbm, vmem)):
        loads[i] = pltpu.make_async_copy(src, dst, load.at[i])
    for i in (0, 3, 2, 4, 6, 1, 7, 5):
        loads[i].start()

    d1 = FIRST_DILATION
    c = sig.shape[1]
    me = lax.axis_index("tm")
    has_prev, has_next = me > 0, me < count - 1
    has_far, has_near = me < count - offset, me >= offset
    nxt, prv = lax.rem(me + 1, count), lax.rem(me + count - 1, count)
    far, near = lax.rem(me + offset, count), lax.rem(me + count - offset, count)

    barrier = pltpu.get_barrier_semaphore()
    peers = sum(there.astype(jnp.int32) for there in (has_prev, has_next, has_far, has_near))
    for there, target in ((has_prev, prv), (has_next, nxt), (has_far, far), (has_near, near)):
        @pl.when(there)
        def _(target=target):
            pl.semaphore_signal(barrier, inc=1, device_id={"tm": target}, device_id_type=MESH)
    if fused:
        _, _, _, partner, plane, column = places(lax.axis_index("dp"), me)
        for target in [partner] + [there for there, _ in plane + column]:
            pl.semaphore_signal(barrier, inc=1, device_id=target, device_id_type=MESH)
        peers = peers + 7
    pl.semaphore_wait(barrier, peers)
    if fused:
        per = refs[23:]
        sum_one = Sum(*per[:7], out1, *per[7:9], scale)
        sum_two = Sum(*per[9:16], out2, *per[16:18], scale)
    else:
        sum_one, sum_two = Local(out1), Local(out2)

    def copy(src, dst, s, r, target):
        return pltpu.make_async_remote_copy(
            src_ref=src, dst_ref=dst, send_sem=s, recv_sem=r, device_id={"tm": target}, device_id_type=MESH
        )

    halo_copy = copy(hbm[0].at[pl.ds(steps - d1, d1)], halo, halo_s, halo_r, nxt)
    mid_copy, a2_copy, a1_copy = [], [], []
    for i, (at, size) in enumerate(chunks):
        rows = pl.ds(at, size)
        mid_copy.append(copy(mid.at[rows], past2.at[rows], mid_s.at[i], mid_r.at[i], far))
        a2_copy.append(copy(ahead2.at[rows], back2.at[rows], a2_s.at[i], a2_r.at[i], near))
        a1_copy.append(copy(ahead1.at[rows], back1.at[rows], a1_s.at[i], a1_r.at[i], prv) if at < d1 else None)

    @pl.when(has_next)
    def _():
        halo_copy.start()

    @pl.when(jnp.logical_not(has_prev))
    def _():
        halo[...] = jnp.zeros_like(halo)

    @pl.when(jnp.logical_not(has_near))
    def _():
        past2[...] = jnp.zeros_like(past2)

    @pl.when(jnp.logical_not(has_far))
    def _():
        back2[...] = jnp.zeros_like(back2)

    @pl.when(jnp.logical_not(has_next))
    def _():
        back1[...] = jnp.zeros_like(back1)

    def past1(at, size):
        return halo[pl.ds(at, size), :] if at < d1 else sig[pl.ds(at - d1, size), :]

    for i in (0, 3, 2, 4):
        loads[i].wait()
    def send_middle(i):
        @pl.when(has_far)
        def _():
            if i >= 2:
                mid_copy[i - 2].wait_send()
            mid_copy[i].start()

    waited_halo = False
    for i, (at, size) in enumerate(chunks):
        rows = pl.ds(at, size)
        if at < d1 and not waited_halo:
            waited_halo = True

            @pl.when(has_prev)
            def _():
                halo_copy.wait_recv()
        u = sig[rows, :]
        pre = mm(past1(at, size), p1[...]) + mm(u, w1[...])
        f = jnp.tanh(pre[:, :c])
        g = sigmoid(pre[:, c:])
        hid = (f * g).astype(BF16)
        f1[rows, :] = f
        g1[rows, :] = g
        h1[rows, :] = hid
        mid[rows, :] = (u.astype(F32) + mm(hid, m1[...])).astype(BF16)

        if i < 2:
            send_middle(i)

    for i in (6, 1, 7, 5):
        loads[i].wait()
    for at, size in chunks:
        rows = pl.ds(at, size)
        pre2[rows, :] = mm(mid[rows, :], w2[...])
        hg2[rows, :] = mm_nt(cot[rows, :], m2[...])
    def second(i):
        at, size = chunks[i]
        rows = pl.ds(at, size)

        @pl.when(has_near)
        def _():
            mid_copy[i].wait_recv()
        up = cot[rows, :]
        pre = mm(past2[rows, :], p2[...]) + pre2[rows, :]
        f = jnp.tanh(pre[:, :c])
        g = sigmoid(pre[:, c:])
        h2[rows, :] = (f * g).astype(BF16)
        hg = hg2[rows, :]
        pg = jnp.concatenate([hg * g * (1.0 - f * f), hg * f * g * (1.0 - g)], axis=1).astype(BF16)
        pg2[rows, :] = pg

        @pl.when(has_near)
        def _():
            ahead2[rows, :] = mm_nt(pg, p2[...]).astype(BF16)
            a2_copy[i].start()
        loc2[rows, :] = up.astype(F32) + mm_nt(pg, w2[...])

    def second_terms(at, size, begin):
        rows = pl.ds(at, size)
        pg = pg2[rows, :]
        sum_two.add(begin, None, mm_tn(mid[rows, :], pg), mm_tn(h2[rows, :], cot[rows, :]))
        if begin:
            sum_two.acc[pl.ds(0, 4 * c), :] = jnp.zeros((4 * c, 128), F32)

        @pl.when(has_near)
        def _():
            sum_two.add(False, mm_tn(past2[rows, :], pg), None, None)

    def first(i):
        at, size = chunks[i]
        rows = pl.ds(at, size)

        @pl.when(has_far)
        def _():
            a2_copy[i].wait_recv()
        up = (loc2[rows, :] + back2[rows, :].astype(F32)).astype(BF16)
        up1[rows, :] = up
        hg = mm_nt(up, m1[...])
        f, g = f1[rows, :], g1[rows, :]
        pg = jnp.concatenate([hg * g * (1.0 - f * f), hg * f * g * (1.0 - g)], axis=1).astype(BF16)
        pg1[rows, :] = pg

    def first_grads(i):
        at, size = chunks[i]
        rows = pl.ds(at, size)
        pg = pg1[rows, :]
        ahead1[rows, :] = mm_nt(pg, p1[...]).astype(BF16)
        if at < d1:
            @pl.when(has_prev)
            def _():
                a1_copy[i].start()
        loc1[rows, :] = up1[rows, :].astype(F32) + mm_nt(pg, w1[...])

    def first_terms(at, size, begin):
        rows = pl.ds(at, size)
        pg = pg1[rows, :]
        sum_one.add(begin, mm_tn(past1(at, size), pg), mm_tn(sig[rows, :], pg), mm_tn(h1[rows, :], up1[rows, :]))

    span = chunks[1][1]
    second(0)
    send_middle(2)
    second(1)
    send_middle(3)
    first(0)
    first_grads(0)
    second_terms(d1, 2 * span, True)
    second(2)
    first(1)
    first_grads(1)
    second_terms(0, span, False)
    second(3)
    second_terms(span, span, False)
    sum_two.send1()
    first(2)
    first_grads(2)
    sum_two.send2()
    first_terms(d1, 2 * span, True)
    first_terms(0, span, False)
    first(3)
    first_terms(span, span, False)
    sum_one.send1()
    sum_two.send3()
    first_grads(3)
    sum_one.send2()
    sum_two.back3()
    sum_two.back2()
    sum_one.send3()
    sum_two.back1()
    sum_one.back3()

    for i, (at, size) in enumerate(chunks):
        if at < d1:
            @pl.when(has_next)
            def _(i=i):
                a1_copy[i].wait_recv()
    rest = steps - d1
    if rest:
        gsig[pl.ds(0, rest), :] = (loc1[pl.ds(0, rest), :] + ahead1[pl.ds(d1, rest), :].astype(F32)).astype(BF16)
    gsig[pl.ds(rest, d1), :] = (loc1[pl.ds(rest, d1), :] + back1[...].astype(F32)).astype(BF16)
    stores[0].start()

    sum_one.back2()
    sum_two.finish()
    unpack(out2, 4)
    sum_one.back1()
    sum_one.finish()
    unpack(out1, 1)
    sum_one.drain()
    sum_two.drain()

    for c in stores:
        c.wait()

    @pl.when(has_next)
    def _():
        halo_copy.wait_send()
    for i in range(len(chunks)):
        if i >= len(chunks) - 2:
            @pl.when(has_far)
            def _(i=i):
                mid_copy[i].wait_send()

        @pl.when(has_near)
        def _(i=i):
            a2_copy[i].wait_send()
        if a1_copy[i] is not None:
            @pl.when(has_prev)
            def _(i=i):
                a1_copy[i].wait_send()


def write(*refs):
    count = len(refs) // 3
    src, dst, (*held, sem) = refs[:count], refs[count : 2 * count], refs[2 * count :]
    inward = [pltpu.make_async_copy(a, b, sem.at[0, i]) for i, (a, b) in enumerate(zip(src, held))]
    outward = [pltpu.make_async_copy(a, b, sem.at[1, i]) for i, (a, b) in enumerate(zip(held, dst))]
    for c in inward:
        c.start()
    for a, b in zip(inward, outward):
        a.wait()
        b.start()
    for c in outward:
        c.wait()


def body(signal, cotangent, p1, w1, m1, p2, w2, m2):
    seqs, steps, c = signal.shape
    count, groups = lax.axis_size("tm"), lax.axis_size("dp")
    gate = p1.shape[1]
    scale = 1.0 / math.sqrt(seqs * groups * steps * count)
    fused = (groups, count) == (2, 16)
    chunks = ((512, 256), (768, 256), (0, 256), (256, 256))
    nch = len(chunks)
    hbm = pl.BlockSpec(memory_space=pltpu.HBM)
    S = jax.ShapeDtypeStruct
    dma = pltpu.SemaphoreType.DMA
    wide = (2 * gate + c) // 128 * c
    packed = S((wide, 128), BF16 if fused else F32)
    args = (signal.reshape(steps, c), cotangent.reshape(steps, c), p1, w1, m1, p2, w2, m2)
    half = wide // 2
    per_sum = [
        pltpu.VMEM((wide, 128), F32),
        pltpu.VMEM((half, 128), BF16),
        pltpu.VMEM((half, 128), BF16),
        pltpu.VMEM((3, half // 4, 128), BF16),
        pltpu.VMEM((3, half // 16, 128), BF16),
        pltpu.VMEM((half, 128), BF16),
        pltpu.VMEM((half // 4, 128), BF16),
        dma((14,)),
        dma((14,)),
    ]
    kind = packed.dtype
    shapes = [S((steps, c), BF16)] + [S((c, gate), kind), S((c, gate), kind), S((c, c), kind)] * 2
    held = [pltpu.VMEM(a.shape, a.dtype) for a in shapes]
    out = pl.pallas_call(
        functools.partial(kernel, count, SECOND_DILATION // steps, steps, chunks, scale, fused),
        out_shape=shapes,
        in_specs=[hbm] * 8,
        out_specs=[hbm] * 7,
        scratch_shapes=[pltpu.VMEM(a.shape, BF16) for a in args]
        + [
            *held,
            pltpu.VMEM(packed.shape, packed.dtype),
            pltpu.VMEM(packed.shape, packed.dtype),
            dma((7,)),
            pltpu.VMEM((FIRST_DILATION, c), BF16),
            pltpu.VMEM((steps, c), F32),
            pltpu.VMEM((steps, c), F32),
            pltpu.VMEM((steps, c), BF16),
            pltpu.VMEM((steps, c), BF16),
            pltpu.VMEM((steps, c), BF16),
            pltpu.VMEM((steps, c), BF16),
            pltpu.VMEM((steps, c), BF16),
            pltpu.VMEM((steps, gate), F32),
            pltpu.VMEM((steps, c), F32),
            pltpu.VMEM((steps, c), F32),
            pltpu.VMEM((steps, c), BF16),
            pltpu.VMEM((FIRST_DILATION, c), BF16),
            pltpu.VMEM((steps, c), F32),
            pltpu.VMEM((steps, c), BF16),
            pltpu.VMEM((steps, c), BF16),
            pltpu.VMEM((steps, gate), BF16),
            pltpu.VMEM((steps, gate), BF16),
            dma((8,)),
            dma, dma,
            dma((nch,)), dma((nch,)), dma((nch,)), dma((nch,)), dma((nch,)), dma((nch,)),
        ]
        + (per_sum * 2 if fused else []),
        compiler_params=pltpu.CompilerParams(
            collective_id=0, has_side_effects=True, vmem_limit_bytes=62 * 1024 * 1024
        ),
        name="layers",
    )(*args)
    if fused:
        out = pl.pallas_call(
            write,
            out_shape=shapes,
            in_specs=[hbm] * 7,
            out_specs=[hbm] * 7,
            scratch_shapes=held + [dma((2, 7))],
            compiler_params=pltpu.CompilerParams(vmem_limit_bytes=62 * 1024 * 1024),
            name="write",
        )(*out)
        grads = tuple(out[1:])
    else:
        grads = tuple((t * scale).astype(BF16) for t in lax.psum(tuple(out[1:]), ("dp", "tm")))
    return (out[0].reshape(signal.shape),) + grads


def solution(mesh):
    in_specs = (P("dp", "tm", None), P("dp", "tm", None), P(), P(), P(), P(), P(), P())
    out_specs = (P("dp", "tm", None), P(), P(), P(), P(), P(), P())
    return jax.shard_map(body, mesh=mesh, in_specs=in_specs, out_specs=out_specs, check_vma=False)
```
